256 devices in a mesh: gx: 4 (over y), gy: 8 (over z_lo, core), gz: 8 (over z_hi, x).
Axes of the slice: x: 4, y: 4, z: 8 (z_hi: 2, z_lo: 4; z = z_hi * 4 + z_lo), core: 2. Of those that a mesh axis runs over, the one named last changes fastest.
Arguments:
- density: float32 [3, 3, 3, 8, 16, 1024], P(None, None, None, 'gx', 'gy', 'gz'), may hold values from 0.5 to 2
- energy: float32 [3, 3, 3, 8, 16, 1024], P(None, None, None, 'gx', 'gy', 'gz'), may hold values from 0.2 to 10
- velocity: float32 [3, 16, 32, 2048], P(None, 'gx', 'gy', 'gz'), may hold values from -3 to 3
Outputs:
- new_velocity: float32 [3, 16, 32, 2048], P(None, 'gx', 'gy', 'gz')
- remapped: float32 [5, 3, 3, 3, 8, 16, 1024], P(None, None, None, None, 'gx', 'gy', 'gz')
The draws below stay inside these ranges and needn't reach their ends.
All inputs are finite; a program needn't handle non-finite values.
Results may differ from the reference program's by a relative error of at most 0.00002.
Values sent between devices are 32-bit elements; how exact they have to be, the bound alone decides.
No kernel may reach another device: no remote copies, remote signals or barrier semaphores. Data moves between devices by JAX's collectives and lax.ppermute only.
A program may use at most 128 MiB of HBM per device.

```python
import math
import jax
import jax.numpy as jnp
from jax import lax

NX = 8
NY = 16
NZ = 1024


def draw_energy(key, part):
    key = jax.random.fold_in(key, 7)
    shape = (3, 3, 3, NX, NY, NZ)
    xs = (jnp.arange(NX, dtype=jnp.float32) / NX).reshape(1, 1, 1, NX, 1, 1)
    ys = (jnp.arange(NY, dtype=jnp.float32) / NY).reshape(1, 1, 1, 1, NY, 1)
    zs = (jnp.arange(NZ, dtype=jnp.float32) / NZ).reshape(1, 1, 1, 1, 1, NZ)
    trend = 0.5 + 4.0 * (xs + ys + zs) / 3.0
    rough = jnp.exp(jax.random.uniform(key, shape, jnp.float32, -0.69, 0.69))
    return (trend * rough).astype(jnp.float32)


def steps_of(key, shape, split, least, largest):
    loudness = 1.0
    for axis_at, blocks in split:
        heights = jax.random.uniform(jax.random.fold_in(jax.random.fold_in(key, 6), axis_at), (blocks,), jnp.float32, least / len(split), largest / len(split))
        loudness = loudness * jnp.repeat(jnp.exp(heights), shape[axis_at] // blocks).reshape((-1,) + (1,) * (len(shape) - 1 - axis_at))
    return loudness


def noise(key, dims, width, bound, cuts=(), held_as=jnp.bfloat16):
    loudness = steps_of(key, dims, cuts, -0.22, 0.18) if cuts else 1.0
    entries = jax.random.normal(key, dims, jnp.float32) * width * loudness
    return jnp.minimum(jnp.maximum(entries, -bound), bound).astype(held_as)


def setup_inputs(seed: int = 0) -> dict:
    arg_keys = jax.random.split(jax.random.key(seed), 4)
    return {
        "density": jnp.clip(jnp.exp(math.log(2.0) - 1.3862944 * jax.random.uniform(arg_keys[0], (3, 3, 3, NX, NY, NZ), jnp.float32) ** steps_of(arg_keys[0], (3, 3, 3, NX, NY, NZ), ((3, 4), (4, 8), (5, 8)), -0.2, 0.2)), 0.5, 2.0),
        "energy": draw_energy(jax.random.fold_in(arg_keys[3], 71), 0),
        "velocity": noise(arg_keys[2], (3, 2 * NX, 2 * NY, 2 * NZ), 0.5, 3.0, ((1, 4), (2, 8), (3, 8)), jnp.float32),
    }


GAMMA = 1.4
CFL = 0.1

def tables():
    root = math.sqrt(0.6)
    points = [0.5 - 0.5 * root, 0.5, 0.5 + 0.5 * root]
    weights = [5.0 / 18.0, 8.0 / 18.0, 5.0 / 18.0]

    def bernstein(t):
        return [(1.0 - t) * (1.0 - t), 2.0 * t * (1.0 - t), t * t]

    def bern_slope(t):
        return [-2.0 * (1.0 - t), 2.0 - 4.0 * t, 2.0 * t]

    def lagrange(a, t):
        result = 1.0
        for m in range(3):
            if m != a:
                result = result * (t - points[m]) / (points[a] - points[m])
        return result

    def lagrange_slope(a, t):
        result = 0.0
        for k in range(3):
            if k != a:
                factor = 1.0 / (points[a] - points[k])
                for m in range(3):
                    if m != a and m != k:
                        factor = factor * (t - points[m]) / (points[a] - points[m])
                result = result + factor
        return result
    return {'eval_b': [[bernstein(points[q])[a] for q in range(3)] for a in range(3)], 'force_b': [[weights[q] * bernstein(points[q])[a] for a in range(3)] for q in range(3)], 'force_d': [[weights[q] * bern_slope(points[q])[a] for a in range(3)] for q in range(3)], 'volume': [[weights[q] * lagrange_slope(a, points[q]) / weights[a] for a in range(3)] for q in range(3)], 'low_trace': [lagrange(a, 0.0) for a in range(3)], 'high_trace': [lagrange(a, 1.0) for a in range(3)], 'low_lift': [lagrange(a, 0.0) / weights[a] for a in range(3)], 'high_lift': [lagrange(a, 1.0) / weights[a] for a in range(3)]}

def contract(source, matrix, position):
    pieces = []
    for j in range(3):
        summed = matrix[0][j] * jnp.take(source, 0, axis=position)
        for i in range(1, 3):
            summed = summed + matrix[i][j] * jnp.take(source, i, axis=position)
        pieces.append(summed)
    return jnp.stack(pieces, axis=position)

def trace_of(source, vector, position):
    summed = vector[0] * jnp.take(source, 0, axis=position)
    for i in range(1, 3):
        summed = summed + vector[i] * jnp.take(source, i, axis=position)
    return summed

def element_parts(density, energy, tables_in):
    pressure = (GAMMA - 1.0) * density * energy
    fb = tables_in['force_b']
    fd = tables_in['force_d']
    force_x = contract(contract(contract(pressure, fd, 0), fb, 1), fb, 2)
    force_y = contract(contract(contract(pressure, fb, 0), fd, 1), fb, 2)
    force_z = contract(contract(contract(pressure, fb, 0), fb, 1), fd, 2)
    mass_part = contract(contract(contract(density, fb, 0), fb, 1), fb, 2)
    return jnp.stack([force_x, force_y, force_z, mass_part], axis=0)

def fold_periodic(parts):
    first = jnp.take(parts, 0, axis=1)
    middle = jnp.take(parts, 1, axis=1)
    last = jnp.take(parts, 2, axis=1)
    even = first + jnp.roll(last, 1, axis=3)
    woven = jnp.stack([even, middle], axis=4)
    shape = woven.shape
    return woven.reshape(shape[:3] + (shape[3] * 2,) + shape[5:])

def unfold_periodic(nodes):
    count = nodes.shape[3]
    even = lax.slice_in_dim(nodes, 0, count, 2, 3)
    odd = lax.slice_in_dim(nodes, 1, count, 2, 3)
    after = jnp.roll(even, -1, axis=3)
    return jnp.stack([even, odd, after], axis=1)

def face_speeds(elem_vel, step_size, tables_in):
    eb = tables_in['eval_b']
    gauss_vel = contract(contract(contract(elem_vel, eb, 1), eb, 2), eb, 3)
    lows = []
    highs = []
    for d in range(3):
        component = elem_vel[d]
        lower = jnp.take(component, 0, axis=d)
        upper = jnp.take(component, 2, axis=d)
        lows.append(-step_size * contract(contract(lower, eb, 0), eb, 1))
        highs.append(-step_size * contract(contract(upper, eb, 0), eb, 1))
    return (gauss_vel, lows, highs)

def rate_terms(conserved, displace, lows, highs, tms, tps, outms, outps, tables_in):
    summed = None
    for d in range(3):
        volume = contract(displace[d][None] * conserved, tables_in['volume'], 1 + d)
        flux_up = jnp.maximum(highs[d], 0.0)[None] * tps[d] + jnp.minimum(highs[d], 0.0)[None] * outps[d]
        flux_down = jnp.maximum(-lows[d], 0.0)[None] * tms[d] + jnp.minimum(-lows[d], 0.0)[None] * outms[d]
        lifted = jnp.stack([-(tables_in['high_lift'][a] * flux_up + tables_in['low_lift'][a] * flux_down) for a in range(3)], axis=1 + d)
        piece = volume + lifted
        summed = piece if summed is None else summed + piece
    return summed

def reference(density, energy, velocity):
    tables_in = tables()
    sound_top = jnp.max(jnp.sqrt(GAMMA * (GAMMA - 1.0) * energy))
    step_size = CFL / sound_top
    parts = element_parts(density, energy, tables_in)
    node_total = fold_periodic(fold_periodic(fold_periodic(parts)))
    new_velocity = velocity + step_size * node_total[0:3] / node_total[3:4]
    elem_vel = unfold_periodic(unfold_periodic(unfold_periodic(new_velocity)))
    gauss_vel, lows, highs = face_speeds(elem_vel, step_size, tables_in)
    displace = -step_size * gauss_vel
    conserved = jnp.stack([density, density * energy, density * gauss_vel[0], density * gauss_vel[1], density * gauss_vel[2]], axis=0)

    def rates(fields):
        tms = [trace_of(fields, tables_in['low_trace'], 1 + d) for d in range(3)]
        tps = [trace_of(fields, tables_in['high_trace'], 1 + d) for d in range(3)]
        outps = [jnp.roll(tms[d], -1, axis=3 + d) for d in range(3)]
        outms = [jnp.roll(tps[d], 1, axis=3 + d) for d in range(3)]
        return rate_terms(fields, displace, lows, highs, tms, tps, outms, outps, tables_in)
    section_one = conserved + rates(conserved)
    section_two = 0.75 * conserved + 0.25 * (section_one + rates(section_one))
    remapped = 1.0 / 3.0 * conserved + 2.0 / 3.0 * (section_two + rates(section_two))
    return (new_velocity, remapped)
```

```python
import functools
import math

import jax
import jax.numpy as jnp
from jax import lax
from jax.experimental import pallas as pl
from jax.experimental.pallas import tpu as pltpu
from jax.sharding import PartitionSpec as P

GAMMA = 1.4
CFL = 0.1
F32 = jnp.float32
TILE = (8, 128)
GROUP = 14


def tables():
    root = math.sqrt(0.6)
    points = [0.5 - 0.5 * root, 0.5, 0.5 + 0.5 * root]
    weights = [5.0 / 18.0, 8.0 / 18.0, 5.0 / 18.0]

    def bernstein(t):
        return [(1.0 - t) * (1.0 - t), 2.0 * t * (1.0 - t), t * t]

    def bern_slope(t):
        return [-2.0 * (1.0 - t), 2.0 - 4.0 * t, 2.0 * t]

    def lagrange(a, t):
        result = 1.0
        for m in range(3):
            if m != a:
                result = result * (t - points[m]) / (points[a] - points[m])
        return result

    def lagrange_slope(a, t):
        result = 0.0
        for k in range(3):
            if k != a:
                factor = 1.0 / (points[a] - points[k])
                for m in range(3):
                    if m != a and m != k:
                        factor = factor * (t - points[m]) / (points[a] - points[m])
                result = result + factor
        return result

    return {
        "eval_b": [[bernstein(points[q])[a] for q in range(3)] for a in range(3)],
        "force_b": [[weights[q] * bernstein(points[q])[a] for a in range(3)] for q in range(3)],
        "force_d": [[weights[q] * bern_slope(points[q])[a] for a in range(3)] for q in range(3)],
        "volume": [
            [weights[q] * lagrange_slope(a, points[q]) / weights[a] for a in range(3)]
            for q in range(3)
        ],
        "low_trace": [lagrange(a, 0.0) for a in range(3)],
        "high_trace": [lagrange(a, 1.0) for a in range(3)],
        "low_lift": [lagrange(a, 0.0) / weights[a] for a in range(3)],
        "high_lift": [lagrange(a, 1.0) / weights[a] for a in range(3)],
    }


TAB = tables()


def row_index():
    return lax.broadcasted_iota(jnp.int32, TILE, 0)


def lane_index():
    return lax.broadcasted_iota(jnp.int32, TILE, 1)


def roll_rows(x, by):
    return pltpu.roll(x, by % 8, 0)


def roll_lanes(x, by):
    by = by % 128
    return x if by == 0 else pltpu.roll(x, by, 1)


class Shifts:
    def __init__(self):
        row = row_index()
        lane = lane_index()
        self.first = {2: (row & 2) == 0, 1: (row & 1) == 0}
        self.top = lane == 127
        self.bottom = lane == 0

    def pack_low(self, a, b, step):
        return a if b is None else jnp.where(self.first[step], a, roll_rows(b, step))

    def pack_high(self, a, b, step):
        return a if b is None else jnp.where(self.first[step], roll_rows(b, -step), a)

    def prev(self, own, packed, second, step):
        outside = packed if second else roll_rows(packed, -step)
        return jnp.where(self.first[step], outside, roll_rows(own, step))

    def next(self, own, packed, second, step):
        outside = packed if second else roll_rows(packed, step)
        return jnp.where(self.first[step], roll_rows(own, -step), outside)

    def z_prev(self, x):
        t = roll_lanes(x, 1)
        return jnp.where(self.bottom, roll_rows(t, 4), t)

    def z_next(self, x):
        t = roll_lanes(x, -1)
        return jnp.where(self.top, roll_rows(t, 4), t)


def combine(values, coefs):
    total = None
    for value, coef in zip(values, coefs):
        if coef == 0.0:
            continue
        term = coef * value
        total = term if total is None else total + term
    return total


def column(matrix, j):
    return [matrix[i][j] for i in range(3)]


def contract(source, matrix, position):
    result = {}
    for key in source:
        if key[position] == 0:
            keys = [key[:position] + (m,) + key[position + 1 :] for m in range(3)]
            for j in range(3):
                result[keys[j]] = combine([source[k] for k in keys], column(matrix, j))
    return result


POINTS = [(a, b, c) for a in range(3) for b in range(3) for c in range(3)]


def point(a, b, c):
    return 9 * a + 3 * b + c


def pack_kernel(dens, ener, vel, to_up, to_down, both, nodes, top, wide, split):
    lane = lane_index()
    low = ener[0, 0]
    for q in range(27):
        for i in range(2):
            both[q, 2 * i : 2 * i + 2, :] = dens[q, i]
            both[q, 4 + 2 * i : 6 + 2 * i, :] = ener[q, i]
            low = jnp.maximum(low, ener[q, i])
    top[...] = jnp.broadcast_to(jnp.max(low, keepdims=True), TILE)
    half = (2 * lane) % 128
    for d in range(3):
        for px in range(2):
            slot = 2 * d + px
            wide[slot, 0:4, :] = vel[d, px]
            wide[slot, 4:8, :] = vel[d, 2 + px]
            left = wide[slot, :, 0:128]
            right = wide[slot, :, 128:256]
            for pz in range(2):
                picked = jnp.where(
                    lane < 64,
                    jnp.take_along_axis(left, half + pz, axis=1),
                    jnp.take_along_axis(right, half + pz, axis=1),
                )
                split[slot, 8 * pz : 8 * pz + 8, :] = picked
            for py in range(2):
                nodes[2 * slot + py] = split[slot, pl.ds(py, 8, stride=2), :]
    sources = [[both[q] for q in range(GROUP)], [both[q] for q in range(GROUP, 27)]]
    sources.append([nodes[n] for n in range(12)])
    for t in range(3):
        up = jnp.ones(TILE, F32)
        down = jnp.ones(TILE, F32)
        for g, tile in enumerate(sources[t]):
            group = lane // 4
            up = jnp.where(group == 2 * g, roll_lanes(tile, 8 * g - 124), up)
            down = jnp.where(group == 2 * g + 1, roll_lanes(tile, 8 * g + 4), down)
        to_up[t] = up
        to_down[t] = down


def force_kernel(both, nodes, from_below, from_above, rho, vz, parts, to_right, to_left):
    sh = Shifts()
    row = row_index()
    own = row < 4
    lane = lane_index()
    merged = [jnp.where((lane & 7) < 4, from_below[t], from_above[t]) for t in range(3)]

    def extend(tile, t, g):
        halo = roll_lanes(merged[t], 124 - 8 * g)
        return (
            jnp.where(own, tile, roll_rows(halo, 4)),
            jnp.where(own, roll_rows(tile, 4), halo),
        )

    density = {}
    pressure = {}
    for key in POINTS:
        q = point(*key)
        dens, ener = extend(both[q], q // GROUP, q % GROUP)
        rho[0, q] = dens
        heat = dens * ener
        rho[1, q] = heat
        density[key] = dens
        pressure[key] = (GAMMA - 1.0) * heat
    for n in range(12):
        even, odd = extend(nodes[n], 2, n)
        vz[2 * n] = even
        vz[2 * n + 1] = odd
    fb = TAB["force_b"]
    fd = TAB["force_d"]
    along_b = contract(pressure, fb, 0)
    along_d = contract(pressure, fd, 0)
    bb = contract(along_b, fb, 1)
    fields = [
        contract(contract(along_d, fb, 1), fb, 2),
        contract(contract(along_b, fd, 1), fb, 2),
        contract(bb, fd, 2),
        contract(contract(contract(density, fb, 0), fb, 1), fb, 2),
    ]
    for f in range(4):
        for a in range(3):
            for b in range(3):
                even = fields[f][a, b, 0] + sh.z_prev(fields[f][a, b, 2])
                odd = fields[f][a, b, 1]
                parts[f, 3 * a + b, 0] = even
                parts[f, 3 * a + b, 1] = odd
                if a == 2:
                    to_right[3 * f + b] = sh.pack_high(even, odd, 2)
                if a == 0:
                    to_left[3 * f + b] = sh.pack_low(even, odd, 2)
    for d in range(3):
        for py in range(2):
            n = 4 * d + py
            to_left[12 + 2 * d + py] = sh.pack_low(vz[2 * n], vz[2 * n + 1], 2)


def rim_kernel(parts, vz, from_left, from_right, sums, ev, to_up, to_down):
    sh = Shifts()
    for f in range(4):
        for b in range(3):
            for z in range(2):
                first = parts[f, b, z]
                last = parts[f, 6 + b, z]
                full = [
                    first + sh.prev(last, from_left[3 * f + b], z, 2),
                    parts[f, 3 + b, z],
                    last + sh.next(first, from_right[3 * f + b], z, 2),
                ]
                for a in range(3):
                    sums[f, 3 * a + b, z] = full[a]
        for a in range(3):
            to_up[3 * f + a] = sh.pack_high(sums[f, 3 * a + 2, 0], sums[f, 3 * a + 2, 1], 1)
            to_down[3 * f + a] = sh.pack_low(sums[f, 3 * a, 0], sums[f, 3 * a, 1], 1)
    for d in range(3):
        for py in range(2):
            for z in range(2):
                first = vz[2 * (4 * d + py) + z]
                ev[d, py, z] = first
                ev[d, 2 + py, z] = vz[2 * (4 * d + 2 + py) + z]
                ev[d, 4 + py, z] = sh.next(first, from_right[12 + 2 * d + py], z, 2)
        for a in range(3):
            to_down[12 + 3 * d + a] = sh.pack_low(ev[d, 2 * a, 0], ev[d, 2 * a, 1], 1)


def face_messages(sh, fields, f, right, left, up, down):
    low = TAB["low_trace"]
    high = TAB["high_trace"]
    for step, over, under in ((2, right, left), (1, up, down)):
        lows = []
        highs = []
        for m in range(3):
            for c in range(3):
                if step == 2:
                    line = [fields[a, m, c] for a in range(3)]
                else:
                    line = [fields[m, b, c] for b in range(3)]
                lows.append(combine(line, low))
                highs.append(combine(line, high))
        lows.append(None)
        highs.append(None)
        for n in range(5):
            over[f, n] = sh.pack_high(highs[2 * n], highs[2 * n + 1], step)
            under[f, n] = sh.pack_low(lows[2 * n], lows[2 * n + 1], step)


def velocity_kernel(
    sums, ev, from_down, from_up, tops, rho,
    new_vel, u0, disp, speeds, right, left, up, down, split, wide,
):
    sh = Shifts()
    lane = lane_index()
    top = tops[0:8]
    for n in range(1, tops.shape[0] // 8):
        top = jnp.maximum(top, tops[8 * n : 8 * n + 8])
    for by in (4, 2, 1):
        top = jnp.maximum(top, roll_rows(top, by))
    step = CFL / jnp.sqrt((GAMMA * (GAMMA - 1.0)) * top)
    vel = [{} for _ in range(3)]
    for a in range(3):
        for z in range(2):
            total = []
            for f in range(4):
                first = sums[f, 3 * a, z]
                last = sums[f, 3 * a + 2, z]
                total.append(
                    [
                        first + sh.prev(last, from_down[3 * f + a], z, 1),
                        sums[f, 3 * a + 1, z],
                        last + sh.next(first, from_up[3 * f + a], z, 1),
                    ]
                )
            scale = [step / total[3][b] for b in range(3)]
            for d in range(3):
                first = ev[d, 2 * a, z]
                old = [
                    first,
                    ev[d, 2 * a + 1, z],
                    sh.next(first, from_up[12 + 3 * d + a], z, 1),
                ]
                for b in range(3):
                    vel[d][a, b, z] = old[b] + total[d][b] * scale[b]
    for d in range(3):
        for px in range(2):
            slot = 2 * d + px
            for py in range(2):
                even = vel[d][px, py, 0]
                odd = vel[d][px, py, 1]
                tile = jnp.where(row_index() < 4, even, roll_rows(odd, 4))
                split[slot, pl.ds(py, 8, stride=2), :] = tile
            even = split[slot, 0:8, :]
            odd = split[slot, 8:16, :]
            for part in range(2):
                at = 64 * part + lane // 2
                wide[slot, :, 128 * part : 128 * part + 128] = jnp.where(
                    (lane & 1) == 0,
                    jnp.take_along_axis(even, at, axis=1),
                    jnp.take_along_axis(odd, at, axis=1),
                )
            new_vel[d, px] = wide[slot, 0:4, :]
            new_vel[d, 2 + px] = wide[slot, 4:8, :]
    eb = TAB["eval_b"]
    minus = -step

    def along_z(even, odd):
        line = [even, odd, sh.z_next(even)]
        return [combine(line, column(eb, q)) for q in range(3)]

    for a, at in ((0, 0), (2, 1)):
        for q in range(3):
            pair = [combine([vel[0][a, b, z] for b in range(3)], column(eb, q)) for z in range(2)]
            for c, value in enumerate(along_z(*pair)):
                speeds[at, 3 * q + c] = minus * value
    gauss = [{} for _ in range(3)]
    for d in range(3):
        across = {}
        for b in range(3):
            for z in range(2):
                line = [vel[d][a, b, z] for a in range(3)]
                for q in range(3):
                    across[q, b, z] = combine(line, column(eb, q))
        if d == 1:
            for b, at in ((0, 2), (2, 3)):
                for q in range(3):
                    for c, value in enumerate(along_z(across[q, b, 0], across[q, b, 1])):
                        speeds[at, 3 * q + c] = minus * value
        for qx in range(3):
            for qy in range(3):
                pair = [
                    combine([across[qx, b, z] for b in range(3)], column(eb, qy)) for z in range(2)
                ]
                if d == 2:
                    speeds[4, 3 * qx + qy] = minus * pair[0]
                for c, value in enumerate(along_z(*pair)):
                    gauss[d][qx, qy, c] = value
                    disp[d, point(qx, qy, c)] = minus * value
    for f in range(5):
        fields = {}
        for key in POINTS:
            q = point(*key)
            if f < 2:
                fields[key] = rho[f, q]
            else:
                fields[key] = rho[0, q] * gauss[f - 2][key]
            u0[f, q] = fields[key]
        face_messages(sh, fields, f, right, left, up, down)


def stage_kernel(weight, last, *refs):
    refs = list(refs)
    u0 = refs.pop(0)
    u = u0 if weight is None else refs.pop(0)
    disp, speeds, from_left, from_right, from_down, from_up = refs[:6]
    outs = refs[6:]
    sh = Shifts()
    low = TAB["low_trace"]
    high = TAB["high_trace"]
    low_lift = TAB["low_lift"]
    high_lift = TAB["high_lift"]
    volume = TAB["volume"]

    def one_field(f, carry):
        fields = {key: u[f, point(*key)] for key in POINTS}
        rate = {}
        for d in range(3):
            for m in range(3):
                for n in range(3):
                    if d == 0:
                        keys = [(a, m, n) for a in range(3)]
                    elif d == 1:
                        keys = [(m, a, n) for a in range(3)]
                    else:
                        keys = [(m, n, a) for a in range(3)]
                    at = 3 * m + n
                    line = [fields[k] for k in keys]
                    moved = [disp[d, point(*k)] * fields[k] for k in keys]
                    tm = combine(line, low)
                    tp = combine(line, high)
                    if d < 2:
                        step = 2 - d
                        under, over = ((from_left, from_right), (from_down, from_up))[d]
                        before = sh.prev(tp, under[f, at // 2], at % 2, step)
                        after = sh.next(tm, over[f, at // 2], at % 2, step)
                        s_low = speeds[2 * d, at]
                        s_high = speeds[2 * d + 1, at]
                        f_low = s_low * jnp.where(s_low > 0.0, before, tm)
                        f_high = s_high * jnp.where(s_high > 0.0, tp, after)
                    else:
                        s_low = speeds[4, at]
                        f_low = s_low * jnp.where(s_low > 0.0, sh.z_prev(tp), tm)
                        f_high = sh.z_next(f_low)
                    for a in range(3):
                        piece = combine(
                            moved + [f_low, f_high],
                            column(volume, a) + [low_lift[a], -high_lift[a]],
                        )
                        rate[keys[a]] = rate[keys[a]] + piece if d else piece
        after = {}
        for key in POINTS:
            q = point(*key)
            if weight is None:
                value = fields[key] + rate[key]
            else:
                value = (1.0 - weight) * u0[f, q] + weight * (fields[key] + rate[key])
            if last:
                outs[0][f, q, 0] = value[0:2]
                outs[0][f, q, 1] = value[2:4]
            else:
                outs[0][f, q] = value
                after[key] = value
        if not last:
            face_messages(sh, after, f, *outs[1:])
        return carry

    lax.fori_loop(0, 5, one_field, 0)


def call(kernel, outs, *args, scratch=(), name=None):
    return pl.pallas_call(
        kernel,
        out_shape=[jax.ShapeDtypeStruct(o, F32) for o in outs],
        in_specs=[pl.BlockSpec(memory_space=pltpu.VMEM)] * len(args),
        out_specs=[pl.BlockSpec(memory_space=pltpu.VMEM)] * len(outs),
        scratch_shapes=[pltpu.VMEM(s, F32) for s in scratch],
        compiler_params=pltpu.CompilerParams(vmem_limit_bytes=32 * 1024 * 1024),
        name=name,
    )(*args)


def send(value, axis, by):
    count = lax.axis_size(axis)
    return lax.ppermute(value, axis, [(i, (i + by) % count) for i in range(count)])


def exchange(right, left, up, down):
    return (
        send(right, "gx", 1),
        send(left, "gx", -1),
        send(up, "gy", 1),
        send(down, "gy", -1),
    )


def shards(density, energy, velocity):
    tile = TILE
    dens = density.reshape((27,) + density.shape[3:])
    ener = energy.reshape((27,) + energy.shape[3:])
    to_up, to_down, both, nodes, top = call(
        pack_kernel,
        [(3,) + tile, (3,) + tile, (27,) + tile, (12,) + tile, tile],
        dens, ener, velocity,
        scratch=[(6, 8, 256), (6, 16, 128)],
        name="pack",
    )
    from_below = send(to_up, "gz", 1)
    from_above = send(to_down, "gz", -1)
    tops = [top] + [send(top, "gx", k) for k in range(1, lax.axis_size("gx"))]
    top = functools.reduce(jnp.maximum, tops)
    peers = lax.axis_size("gy") * lax.axis_size("gz")
    spread = jnp.broadcast_to(top[0:1], (peers, 128))
    tops = lax.all_to_all(spread, ("gy", "gz"), 0, 0, tiled=True)
    rho, vz, parts, to_right, to_left = call(
        force_kernel,
        [(2, 27) + tile, (24,) + tile, (4, 9, 2) + tile, (12,) + tile, (18,) + tile],
        both, nodes, from_below, from_above,
        name="force",
    )
    from_left = send(to_right, "gx", 1)
    from_right = send(to_left, "gx", -1)
    sums, ev, to_up, to_down = call(
        rim_kernel,
        [(4, 9, 2) + tile, (3, 6, 2) + tile, (12,) + tile, (21,) + tile],
        parts, vz, from_left, from_right,
        name="rim",
    )
    from_down = send(to_up, "gy", 1)
    from_up = send(to_down, "gy", -1)
    faces = [(5, 5) + tile] * 4
    state = (5, 27) + tile
    new_velocity, u0, disp, speeds, *messages = call(
        velocity_kernel,
        [velocity.shape, state, (3, 27) + tile, (5, 9) + tile] + faces,
        sums, ev, from_down, from_up, tops, rho,
        scratch=[(6, 16, 128), (6, 8, 256)],
        name="velocity",
    )
    one, *messages = call(
        functools.partial(stage_kernel, None, False), [state] + faces,
        u0, disp, speeds, *exchange(*messages),
        name="stage_one",
    )
    two, *messages = call(
        functools.partial(stage_kernel, 0.25, False), [state] + faces,
        u0, one, disp, speeds, *exchange(*messages),
        name="stage_two",
    )
    (remapped,) = call(
        functools.partial(stage_kernel, 2.0 / 3.0, True), [(5, 27) + density.shape[3:]],
        u0, two, disp, speeds, *exchange(*messages),
        name="stage_three",
    )
    return new_velocity, remapped.reshape((5, 3, 3, 3) + density.shape[3:])


def solution(mesh):
    return jax.shard_map(
        shards,
        mesh=mesh,
        in_specs=(
            P(None, None, None, "gx", "gy", "gz"),
            P(None, None, None, "gx", "gy", "gz"),
            P(None, "gx", "gy", "gz"),
        ),
        out_specs=(P(None, "gx", "gy", "gz"), P(None, None, None, None, "gx", "gy", "gz")),
        check_vma=False,
    )
```

```python
import functools
import math

import jax
import jax.numpy as jnp
from jax import lax
from jax.experimental import pallas as pl
from jax.experimental.pallas import tpu as pltpu
from jax.sharding import Mesh
from jax.sharding import PartitionSpec as P

GAMMA = 1.4
CFL = 0.1
F32 = jnp.float32
TILE = (8, 128)
GX = ("gx",)
GY = ("zl", "co")
GZ = ("zh", "xx")
FLAT = ("gx", "xx")
DEEP = ("zl", "co", "zh")
WEIGHT = pl.CostEstimate(flops=10**11, bytes_accessed=10**8, transcendentals=0)
GROUP = 14


def tables():
    root = math.sqrt(0.6)
    points = [0.5 - 0.5 * root, 0.5, 0.5 + 0.5 * root]
    weights = [5.0 / 18.0, 8.0 / 18.0, 5.0 / 18.0]

    def bernstein(t):
        return [(1.0 - t) * (1.0 - t), 2.0 * t * (1.0 - t), t * t]

    def bern_slope(t):
        return [-2.0 * (1.0 - t), 2.0 - 4.0 * t, 2.0 * t]

    def lagrange(a, t):
        result = 1.0
        for m in range(3):
            if m != a:
                result = result * (t - points[m]) / (points[a] - points[m])
        return result

    def lagrange_slope(a, t):
        result = 0.0
        for k in range(3):
            if k != a:
                factor = 1.0 / (points[a] - points[k])
                for m in range(3):
                    if m != a and m != k:
                        factor = factor * (t - points[m]) / (points[a] - points[m])
                result = result + factor
        return result

    return {
        "eval_b": [[bernstein(points[q])[a] for q in range(3)] for a in range(3)],
        "force_b": [[weights[q] * bernstein(points[q])[a] for a in range(3)] for q in range(3)],
        "force_d": [[weights[q] * bern_slope(points[q])[a] for a in range(3)] for q in range(3)],
        "volume": [
            [weights[q] * lagrange_slope(a, points[q]) / weights[a] for a in range(3)]
            for q in range(3)
        ],
        "low_trace": [lagrange(a, 0.0) for a in range(3)],
        "high_trace": [lagrange(a, 1.0) for a in range(3)],
        "low_lift": [lagrange(a, 0.0) / weights[a] for a in range(3)],
        "high_lift": [lagrange(a, 1.0) / weights[a] for a in range(3)],
    }


TAB = tables()


def row_index():
    return lax.broadcasted_iota(jnp.int32, TILE, 0)


def lane_index():
    return lax.broadcasted_iota(jnp.int32, TILE, 1)


def roll_rows(x, by):
    return pltpu.roll(x, by % 8, 0)


def roll_lanes(x, by):
    by = by % 128
    return x if by == 0 else pltpu.roll(x, by, 1)


class Shifts:
    def __init__(self):
        row = row_index()
        lane = lane_index()
        self.first = {2: (row & 2) == 0, 1: (row & 1) == 0}
        self.own = row < 4
        self.top = lane == 127
        self.bottom = lane == 0

    def pack_low(self, a, b, step):
        return a if b is None else jnp.where(self.first[step], a, roll_rows(b, step))

    def pack_high(self, a, b, step):
        return a if b is None else jnp.where(self.first[step], roll_rows(b, -step), a)

    def prev(self, own, packed, second, step):
        outside = packed if second else roll_rows(packed, -step)
        return jnp.where(self.first[step], outside, roll_rows(own, step))

    def next(self, own, packed, second, step):
        outside = packed if second else roll_rows(packed, step)
        return jnp.where(self.first[step], roll_rows(own, -step), outside)

    def beside(self, over, under, step):
        return jnp.where(self.first[step], over, under)

    def before(self, first_from, second_from, step):
        return jnp.where(
            self.first[step], roll_rows(first_from, -step), roll_rows(second_from, step)
        )

    def z_prev(self, x):
        t = roll_lanes(x, 1)
        return jnp.where(self.bottom, roll_rows(t, 4), t)

    def z_next(self, x):
        t = roll_lanes(x, -1)
        return jnp.where(self.top, roll_rows(t, 4), t)


def combine(values, coefs):
    total = None
    for value, coef in zip(values, coefs):
        if coef == 0.0:
            continue
        term = coef * value
        total = term if total is None else total + term
    return total


def column(matrix, j):
    return [matrix[i][j] for i in range(3)]


def contract(source, matrix, position):
    result = {}
    for key in source:
        if key[position] == 0:
            keys = [key[:position] + (m,) + key[position + 1 :] for m in range(3)]
            for j in range(3):
                result[keys[j]] = combine([source[k] for k in keys], column(matrix, j))
    return result


def message_size(halves):
    tiles = -(-halves // 2)
    return -(-tiles // 2) + -(-tiles // 32)


def write_message(sh, ref, values, high, step):
    values = list(values)
    if len(values) % 2:
        values.append(None)
    pack = sh.pack_high if high else sh.pack_low
    tiles = [pack(values[n], values[n + 1], step) for n in range(0, len(values), 2)]
    group = lane_index() // 8
    base = -(-len(tiles) // 2)
    halos = []
    for n, tile in enumerate(tiles):
        moved = roll_lanes(tile, 8 * (n % 16) + 4)
        if n % 16 == 0:
            halos.append(moved)
        else:
            halos[-1] = jnp.where(group == n % 16, moved, halos[-1])
    if len(tiles) % 2:
        tiles.append(tiles[-1])
    if len(halos) % 2:
        halos.append(halos[-1])
    for n in range(0, len(tiles), 2):
        ref[n // 2] = jnp.where(sh.own, tiles[n], roll_rows(tiles[n + 1], 4))
    for n in range(0, len(halos), 2):
        ref[base + n // 2] = jnp.where(sh.own, roll_rows(halos[n], 4), halos[n + 1])


def read_message(sh, ref, keys, high, step):
    places = {key: n for n, key in enumerate(keys)}
    base = -(-(-(-len(keys) // 2)) // 2)

    def get(key):
        n, odd = divmod(places[key], 2)
        main = ref[n // 2]
        if n % 2:
            main = roll_rows(main, 4)
        halo = ref[base + n // 32]
        if n // 16 % 2 == 0:
            halo = roll_rows(halo, 4)
        tile = jnp.where(sh.own, main, roll_lanes(halo, 124 - 8 * (n % 16)))
        if odd:
            tile = roll_rows(tile, step if high else -step)
        return tile

    return get


FIELDS = range(4)
TRIPLE = range(3)
PAIR = range(2)


def x_keys(high):
    keys = [("sum", f, a, b, z) for f in FIELDS for a in TRIPLE for b in TRIPLE for z in PAIR]
    nodes = 2 if high else 3
    keys += [("old", d, a, p, z) for d in TRIPLE for a in range(nodes) for p in PAIR for z in PAIR]
    return keys + side_keys()


def side_keys():
    keys = [("rho",) + key for key in POINTS]
    return keys + [("heat", m, n) for m in TRIPLE for n in TRIPLE]


def y_keys(high):
    keys = [("sum", f, a, b, z) for f in FIELDS for a in TRIPLE for b in TRIPLE for z in PAIR]
    keys += [("side", f, a, z) for f in FIELDS for a in TRIPLE for z in PAIR]
    nodes = 2 if high else 3
    keys += [("old", d, a, b, z) for d in TRIPLE for a in TRIPLE for b in range(nodes) for z in PAIR]
    if not high:
        keys += [("old_side", d, a, z) for d in TRIPLE for a in TRIPLE for z in PAIR]
    return keys + side_keys()


def side_values(rho, direction, trace):
    values = {("rho",) + key: rho[0, point(*key)] for key in POINTS}
    for m in TRIPLE:
        for n in TRIPLE:
            keys = [(a, m, n) if direction == 0 else (m, a, n) for a in TRIPLE]
            values["heat", m, n] = combine([rho[1, point(*k)] for k in keys], trace)
    return values


POINTS = [(a, b, c) for a in range(3) for b in range(3) for c in range(3)]


def point(a, b, c):
    return 9 * a + 3 * b + c


def pack_kernel(dens, ener, vel, to_up, to_down, both, nodes, top, wide, split):
    lane = lane_index()
    low = ener[0, 0]
    for q in range(27):
        for i in range(2):
            both[q, 2 * i : 2 * i + 2, :] = dens[q, i]
            both[q, 4 + 2 * i : 6 + 2 * i, :] = ener[q, i]
            low = jnp.maximum(low, ener[q, i])
    top[...] = jnp.broadcast_to(jnp.max(low, keepdims=True), top.shape)
    half = (2 * lane) % 128
    for d in range(3):
        for px in range(2):
            slot = 2 * d + px
            wide[slot, 0:4, :] = vel[d, px]
            wide[slot, 4:8, :] = vel[d, 2 + px]
            left = wide[slot, :, 0:128]
            right = wide[slot, :, 128:256]
            for pz in range(2):
                picked = jnp.where(
                    lane < 64,
                    jnp.take_along_axis(left, half + pz, axis=1),
                    jnp.take_along_axis(right, half + pz, axis=1),
                )
                split[slot, 8 * pz : 8 * pz + 8, :] = picked
            for py in range(2):
                nodes[2 * slot + py] = split[slot, pl.ds(py, 8, stride=2), :]
    sources = [[both[q] for q in range(GROUP)], [both[q] for q in range(GROUP, 27)]]
    sources.append([nodes[n] for n in range(12)])
    for t in range(3):
        up = jnp.ones(TILE, F32)
        down = jnp.ones(TILE, F32)
        for g, tile in enumerate(sources[t]):
            group = lane // 4
            up = jnp.where(group == 2 * g, roll_lanes(tile, 8 * g - 124), up)
            down = jnp.where(group == 2 * g + 1, roll_lanes(tile, 8 * g + 4), down)
        to_up[t] = up
        to_down[t] = down


def top_kernel(tops, spread):
    spread[...] = jnp.broadcast_to(jnp.max(tops[...], axis=0, keepdims=True), spread.shape)


def step_kernel(tops, step):
    top = jnp.broadcast_to(jnp.max(tops[...], axis=0, keepdims=True), TILE)
    step[...] = CFL / jnp.sqrt((GAMMA * (GAMMA - 1.0)) * top)


def force_kernel(both, nodes, from_below, from_above, rho, vz, parts, to_right, to_left):
    sh = Shifts()
    lane = lane_index()
    merged = [jnp.where((lane & 7) < 4, from_below[t], from_above[t]) for t in range(3)]

    def extend(tile, t, g):
        halo = roll_lanes(merged[t], 124 - 8 * g)
        return (
            jnp.where(sh.own, tile, roll_rows(halo, 4)),
            jnp.where(sh.own, roll_rows(tile, 4), halo),
        )

    density = {}
    pressure = {}
    for key in POINTS:
        q = point(*key)
        dens, ener = extend(both[q], q // GROUP, q % GROUP)
        heat = dens * ener
        rho[0, q] = dens
        rho[1, q] = heat
        density[key] = dens
        pressure[key] = (GAMMA - 1.0) * heat
    for n in range(12):
        even, odd = extend(nodes[n], 2, n)
        vz[n, 0] = even
        vz[n, 1] = odd
    fb = TAB["force_b"]
    fd = TAB["force_d"]
    along_b = contract(pressure, fb, 0)
    along_d = contract(pressure, fd, 0)
    bb = contract(along_b, fb, 1)
    fields = [
        contract(contract(along_d, fb, 1), fb, 2),
        contract(contract(along_b, fd, 1), fb, 2),
        contract(bb, fd, 2),
        contract(contract(contract(density, fb, 0), fb, 1), fb, 2),
    ]
    for f in FIELDS:
        for a in TRIPLE:
            for b in TRIPLE:
                parts[f, 3 * a + b, 0] = fields[f][a, b, 0] + sh.z_prev(fields[f][a, b, 2])
                parts[f, 3 * a + b, 1] = fields[f][a, b, 1]
    for high, ref, trace in ((True, to_right, "high_trace"), (False, to_left, "low_trace")):
        values = side_values(rho, 0, TAB[trace])
        for f in FIELDS:
            for b in TRIPLE:
                for z in PAIR:
                    line = [parts[f, 3 * a + b, z] for a in TRIPLE]
                    if high:
                        line[0] = line[0] + roll_rows(line[2], 2)
                    else:
                        line[2] = line[2] + roll_rows(line[0], -2)
                    for a in TRIPLE:
                        values["sum", f, a, b, z] = line[a]
        for d in TRIPLE:
            for p in PAIR:
                for z in PAIR:
                    first = vz[4 * d + p, z]
                    values["old", d, 0, p, z] = first
                    values["old", d, 1, p, z] = vz[4 * d + 2 + p, z]
                    values["old", d, 2, p, z] = roll_rows(first, -2)
        write_message(sh, ref, [values[key] for key in x_keys(high)], high, 2)


def assemble(sh, own, side, step):
    inner = [own[0] + sh.before(side[2], own[2], step), own[1], own[2] + sh.before(own[0], side[0], step)]
    outer = [
        jnp.where(sh.first[step], side[0] + roll_rows(own[2], -step), side[0]),
        side[1],
        jnp.where(sh.first[step], side[2], side[2] + roll_rows(own[0], step)),
    ]
    return inner, outer


def rim_kernel(
    parts, vz, rho, from_left, from_right,
    sums, sums_x, old, old_x, rho_x, heat_x, to_up, to_down,
):
    sh = Shifts()
    left = read_message(sh, from_left, x_keys(True), True, 2)
    right = read_message(sh, from_right, x_keys(False), False, 2)

    def beside(*key):
        return sh.beside(right(key), left(key), 2)

    for f in FIELDS:
        for b in TRIPLE:
            for z in PAIR:
                own = [parts[f, 3 * a + b, z] for a in TRIPLE]
                side = [beside("sum", f, a, b, z) for a in TRIPLE]
                inner, outer = assemble(sh, own, side, 2)
                for a in TRIPLE:
                    sums[f, 3 * a + b, z] = inner[a]
                    sums_x[f, 3 * a + b, z] = outer[a]
    for d in TRIPLE:
        for p in PAIR:
            for z in PAIR:
                first = vz[4 * d + p, z]
                beyond = beside("old", d, 0, p, z)
                old[d, p, z] = first
                old[d, 2 + p, z] = vz[4 * d + 2 + p, z]
                old[d, 4 + p, z] = sh.before(first, beyond, 2)
                old_x[d, p, z] = beyond
                old_x[d, 2 + p, z] = beside("old", d, 1, p, z)
                old_x[d, 4 + p, z] = sh.beside(right(("old", d, 2, p, z)), roll_rows(first, 2), 2)
    for key in POINTS:
        rho_x[point(*key)] = beside("rho", *key)
    for m in TRIPLE:
        for n in TRIPLE:
            heat_x[3 * m + n] = beside("heat", m, n)
    for high, ref, trace in ((True, to_up, "high_trace"), (False, to_down, "low_trace")):
        values = side_values(rho, 1, TAB[trace])
        for f in FIELDS:
            for a in TRIPLE:
                for z in PAIR:
                    line = [sums[f, 3 * a + b, z] for b in TRIPLE]
                    if high:
                        line[0] = line[0] + roll_rows(line[2], 1)
                    else:
                        line[2] = line[2] + roll_rows(line[0], -1)
                    for b in TRIPLE:
                        values["sum", f, a, b, z] = line[b]
                    values["side", f, a, z] = sums_x[f, 3 * a + (2 if high else 0), z]
        for d in TRIPLE:
            for a in TRIPLE:
                for z in PAIR:
                    first = old[d, 2 * a, z]
                    values["old", d, a, 0, z] = first
                    values["old", d, a, 1, z] = old[d, 2 * a + 1, z]
                    values["old", d, a, 2, z] = roll_rows(first, -1)
                    values["old_side", d, a, z] = old_x[d, 2 * a, z]
        write_message(sh, ref, [values[key] for key in y_keys(high)], high, 1)


def face_messages(sh, fields, f, right, left, up, down):
    low = TAB["low_trace"]
    high = TAB["high_trace"]
    for step, over, under in ((2, right, left), (1, up, down)):
        lows = []
        highs = []
        for m in range(3):
            for c in range(3):
                if step == 2:
                    line = [fields[a, m, c] for a in range(3)]
                else:
                    line = [fields[m, b, c] for b in range(3)]
                lows.append(combine(line, low))
                highs.append(combine(line, high))
        lows.append(None)
        highs.append(None)
        for n in range(5):
            over[f, n] = sh.pack_high(highs[2 * n], highs[2 * n + 1], step)
            under[f, n] = sh.pack_low(lows[2 * n], lows[2 * n + 1], step)


def velocity_kernel(
    scale, sums, sums_x, old, old_x, rho, rho_x, heat_x, from_down, from_up,
    new_vel, u0, disp, speeds, sides, split, wide,
):
    sh = Shifts()
    lane = lane_index()
    step = scale[...]
    down = read_message(sh, from_down, y_keys(True), True, 1)
    up = read_message(sh, from_up, y_keys(False), False, 1)

    def beside(*key):
        return sh.beside(up(key), down(key), 1)

    centre = [{} for _ in TRIPLE]
    side_x = [{} for _ in TRIPLE]
    side_y = [{} for _ in TRIPLE]
    for a in TRIPLE:
        for z in PAIR:
            total = []
            for f in FIELDS:
                own = [sums[f, 3 * a + b, z] for b in TRIPLE]
                inner, outer = assemble(sh, own, [beside("sum", f, a, b, z) for b in TRIPLE], 1)
                aside = [sums_x[f, 3 * a + b, z] for b in TRIPLE]
                aside = [
                    aside[0] + sh.before(down(("side", f, a, z)), aside[2], 1),
                    aside[1],
                    aside[2] + sh.before(aside[0], up(("side", f, a, z)), 1),
                ]
                total.append((inner, aside, outer))
            for d in TRIPLE:
                first = old[d, 2 * a, z]
                first_x = old_x[d, 2 * a, z]
                beyond = beside("old", d, a, 0, z)
                olds = (
                    [first, old[d, 2 * a + 1, z], sh.before(first, beyond, 1)],
                    [
                        first_x,
                        old_x[d, 2 * a + 1, z],
                        sh.before(first_x, up(("old_side", d, a, z)), 1),
                    ],
                    [
                        beyond,
                        beside("old", d, a, 1, z),
                        sh.beside(up(("old", d, a, 2, z)), roll_rows(first, 1), 1),
                    ],
                )
                for kind, target in enumerate((centre, side_x, side_y)):
                    for b in TRIPLE:
                        over_mass = step / total[3][kind][b]
                        target[d][a, b, z] = olds[kind][b] + total[d][kind][b] * over_mass
    vel = centre
    for d in range(3):
        for px in range(2):
            slot = 2 * d + px
            for py in range(2):
                even = vel[d][px, py, 0]
                odd = vel[d][px, py, 1]
                tile = jnp.where(row_index() < 4, even, roll_rows(odd, 4))
                split[slot, pl.ds(py, 8, stride=2), :] = tile
            even = split[slot, 0:8, :]
            odd = split[slot, 8:16, :]
            for part in range(2):
                at = 64 * part + lane // 2
                wide[slot, :, 128 * part : 128 * part + 128] = jnp.where(
                    (lane & 1) == 0,
                    jnp.take_along_axis(even, at, axis=1),
                    jnp.take_along_axis(odd, at, axis=1),
                )
            new_vel[d, px] = wide[slot, 0:4, :]
            new_vel[d, 2 + px] = wide[slot, 4:8, :]
    eb = TAB["eval_b"]
    minus = -step

    def along_z(even, odd):
        line = [even, odd, sh.z_next(even)]
        return [combine(line, column(eb, q)) for q in range(3)]

    def at_points(nodes, own):
        gauss = [{} for _ in range(3)]
        for d in range(3):
            across = {}
            for b in range(3):
                for z in range(2):
                    line = [nodes[d][a, b, z] for a in range(3)]
                    for q in range(3):
                        across[q, b, z] = combine(line, column(eb, q))
            if d == 1 and own:
                for b, at in ((0, 2), (2, 3)):
                    for q in range(3):
                        for c, value in enumerate(along_z(across[q, b, 0], across[q, b, 1])):
                            speeds[at, 3 * q + c] = minus * value
            for qx in range(3):
                for qy in range(3):
                    pair = [
                        combine([across[qx, b, z] for b in range(3)], column(eb, qy))
                        for z in range(2)
                    ]
                    if d == 2 and own:
                        speeds[4, 3 * qx + qy] = minus * pair[0]
                    for c, value in enumerate(along_z(*pair)):
                        gauss[d][qx, qy, c] = value
                        if own:
                            disp[d, point(qx, qy, c)] = minus * value
        return gauss

    for a, at in ((0, 0), (2, 1)):
        for q in range(3):
            pair = [combine([vel[0][a, b, z] for b in range(3)], column(eb, q)) for z in range(2)]
            for c, value in enumerate(along_z(*pair)):
                speeds[at, 3 * q + c] = minus * value
    gauss = at_points(centre, True)
    for q in range(27):
        u0[0, q] = rho[0, q]
        u0[1, q] = rho[1, q]
    for d in range(3):
        for key in POINTS:
            u0[2 + d, point(*key)] = rho[0, point(*key)] * gauss[d][key]
    low = TAB["low_trace"]
    high = TAB["high_trace"]
    for side, nodes in enumerate((side_x, side_y)):
        turn = 2 - side
        gauss = at_points(nodes, False)
        trace = [jnp.where(sh.first[turn], low[a], high[a]) for a in TRIPLE]
        weigh = {}
        for key in POINTS:
            dens = beside("rho", *key) if side else rho_x[point(*key)]
            weigh[key] = trace[key[side]] * dens
        for m in TRIPLE:
            for n in TRIPLE:
                keys = [(a, m, n) if side == 0 else (m, a, n) for a in TRIPLE]
                at = 3 * m + n
                sides[side, 0, at] = weigh[keys[0]] + weigh[keys[1]] + weigh[keys[2]]
                sides[side, 1, at] = beside("heat", m, n) if side else heat_x[at]
                for d in TRIPLE:
                    sides[side, 2 + d, at] = sum(weigh[k] * gauss[d][k] for k in keys)


def stage_kernel(weight, last, *refs):
    refs = list(refs)
    u0 = refs.pop(0)
    u = u0 if weight is None else refs.pop(0)
    disp, speeds = refs[:2]
    if weight is None:
        (sides,) = refs[2:3]
        outs = refs[3:]
    else:
        from_left, from_right, from_down, from_up = refs[2:6]
        outs = refs[6:]
    sh = Shifts()
    low = TAB["low_trace"]
    high = TAB["high_trace"]
    low_lift = TAB["low_lift"]
    high_lift = TAB["high_lift"]
    volume = TAB["volume"]

    def one_field(f, carry):
        fields = {key: u[f, point(*key)] for key in POINTS}
        rate = {}
        for d in range(3):
            for m in range(3):
                for n in range(3):
                    if d == 0:
                        keys = [(a, m, n) for a in range(3)]
                    elif d == 1:
                        keys = [(m, a, n) for a in range(3)]
                    else:
                        keys = [(m, n, a) for a in range(3)]
                    at = 3 * m + n
                    line = [fields[k] for k in keys]
                    moved = [disp[d, point(*k)] * fields[k] for k in keys]
                    tm = combine(line, low)
                    tp = combine(line, high)
                    if d < 2:
                        step = 2 - d
                        if weight is None:
                            before = sh.before(sides[d, f, at], tp, step)
                            after = sh.before(tm, sides[d, f, at], step)
                        else:
                            under, over = ((from_left, from_right), (from_down, from_up))[d]
                            before = sh.prev(tp, under[f, at // 2], at % 2, step)
                            after = sh.next(tm, over[f, at // 2], at % 2, step)
                        s_low = speeds[2 * d, at]
                        s_high = speeds[2 * d + 1, at]
                        f_low = s_low * jnp.where(s_low > 0.0, before, tm)
                        f_high = s_high * jnp.where(s_high > 0.0, tp, after)
                    else:
                        s_low = speeds[4, at]
                        f_low = s_low * jnp.where(s_low > 0.0, sh.z_prev(tp), tm)
                        f_high = sh.z_next(f_low)
                    for a in range(3):
                        piece = combine(
                            moved + [f_low, f_high],
                            column(volume, a) + [low_lift[a], -high_lift[a]],
                        )
                        rate[keys[a]] = rate[keys[a]] + piece if d else piece
        after = {}
        for key in POINTS:
            q = point(*key)
            if weight is None:
                value = fields[key] + rate[key]
            else:
                value = (1.0 - weight) * u0[f, q] + weight * (fields[key] + rate[key])
            if last:
                outs[0][f, q, 0] = value[0:2]
                outs[0][f, q, 1] = value[2:4]
            else:
                outs[0][f, q] = value
                after[key] = value
        if not last:
            face_messages(sh, after, f, *outs[1:])
        return carry

    lax.fori_loop(0, 5, one_field, 0)


def call(kernel, outs, *args, scratch=(), name=None, weigh=None):
    return pl.pallas_call(
        kernel,
        out_shape=[jax.ShapeDtypeStruct(o, F32) for o in outs],
        in_specs=[pl.BlockSpec(memory_space=pltpu.VMEM)] * len(args),
        out_specs=[pl.BlockSpec(memory_space=pltpu.VMEM)] * len(outs),
        scratch_shapes=[pltpu.VMEM(s, F32) for s in scratch],
        compiler_params=pltpu.CompilerParams(vmem_limit_bytes=32 * 1024 * 1024),
        cost_estimate=weigh,
        name=name,
    )(*args)


def axis_count(axes):
    return math.prod(lax.axis_size(axis) for axis in axes)


def send(value, axis, by):
    count = axis_count(axis)
    return lax.ppermute(value, axis, [(i, (i + by) % count) for i in range(count)])


def exchange(right, left, up, down):
    return (
        send(right, GX, 1),
        send(left, GX, -1),
        send(up, GY, 1),
        send(down, GY, -1),
    )


def shards(density, energy, velocity):
    tile = TILE
    dens = density.reshape((27,) + density.shape[3:])
    ener = energy.reshape((27,) + energy.shape[3:])
    to_up, to_down, both, nodes, top = call(
        pack_kernel,
        [(3,) + tile, (3,) + tile, (27,) + tile, (12,) + tile, (axis_count(FLAT), 128)],
        dens, ener, velocity,
        scratch=[(6, 8, 256), (6, 16, 128)],
        name="pack",
    )
    from_below = send(to_up, GZ, 1)
    from_above = send(to_down, GZ, -1)
    tops = lax.all_to_all(top, FLAT, 0, 0, tiled=True)
    (top,) = call(top_kernel, [(axis_count(DEEP), 128)], tops, name="top", weigh=WEIGHT)
    tops = lax.all_to_all(top, DEEP, 0, 0, tiled=True)
    (step,) = call(step_kernel, [tile], tops, name="step", weigh=WEIGHT)
    parts_shape = (4, 9, 2) + tile
    old_shape = (3, 6, 2) + tile
    rho, vz, parts, to_right, to_left = call(
        force_kernel,
        [
            (2, 27) + tile, (12, 2) + tile, parts_shape,
            (message_size(len(x_keys(True))),) + tile,
            (message_size(len(x_keys(False))),) + tile,
        ],
        both, nodes, from_below, from_above,
        name="force",
    )
    from_left = send(to_right, GX, 1)
    from_right = send(to_left, GX, -1)
    sums, sums_x, old, old_x, rho_x, heat_x, to_up, to_down = call(
        rim_kernel,
        [
            parts_shape, parts_shape, old_shape, old_shape, (27,) + tile, (9,) + tile,
            (message_size(len(y_keys(True))),) + tile,
            (message_size(len(y_keys(False))),) + tile,
        ],
        parts, vz, rho, from_left, from_right,
        name="rim",
    )
    from_down = send(to_up, GY, 1)
    from_up = send(to_down, GY, -1)
    faces = [(5, 5) + tile] * 4
    state = (5, 27) + tile
    new_velocity, u0, disp, speeds, sides = call(
        velocity_kernel,
        [velocity.shape, state, (3, 27) + tile, (5, 9) + tile, (2, 5, 9) + tile],
        step, sums, sums_x, old, old_x, rho, rho_x, heat_x, from_down, from_up,
        scratch=[(6, 16, 128), (6, 8, 256)],
        name="velocity",
    )
    one, *messages = call(
        functools.partial(stage_kernel, None, False), [state] + faces,
        u0, disp, speeds, sides,
        name="stage_one",
    )
    two, *messages = call(
        functools.partial(stage_kernel, 0.25, False), [state] + faces,
        u0, one, disp, speeds, *exchange(*messages),
        name="stage_two",
    )
    (remapped,) = call(
        functools.partial(stage_kernel, 2.0 / 3.0, True), [(5, 27) + density.shape[3:]],
        u0, two, disp, speeds, *exchange(*messages),
        name="stage_three",
    )
    return new_velocity, remapped.reshape((5, 3, 3, 3) + density.shape[3:])


def solution(mesh):
    across, high, deep = (mesh.shape[axis] for axis in ("gx", "gy", "gz"))
    devices = mesh.devices.reshape(across, high // 2, 2, 2, deep // 2)
    return jax.shard_map(
        shards,
        mesh=Mesh(devices, GX + GY + GZ),
        in_specs=(
            P(None, None, None, GX, GY, GZ),
            P(None, None, None, GX, GY, GZ),
            P(None, GX, GY, GZ),
        ),
        out_specs=(P(None, GX, GY, GZ), P(None, None, None, None, GX, GY, GZ)),
        check_vma=False,
    )
```

```python
import functools
import math

import jax
import jax.numpy as jnp
from jax import lax
from jax.experimental import pallas as pl
from jax.experimental.pallas import tpu as pltpu
from jax.sharding import Mesh
from jax.sharding import PartitionSpec as P

GAMMA = 1.4
CFL = 0.1
F32 = jnp.float32
TILE = (8, 128)
GX = ("gx",)
GY = ("zl", "co")
GZ = ("zh", "xx")
FLAT = ("gx", "xx")
DEEP = ("zl", "co", "zh")
FIRST, SECOND = FLAT, DEEP
WEIGHT = pl.CostEstimate(flops=10**11, bytes_accessed=10**8, transcendentals=0)
GROUP = 14


def tables():
    root = math.sqrt(0.6)
    points = [0.5 - 0.5 * root, 0.5, 0.5 + 0.5 * root]
    weights = [5.0 / 18.0, 8.0 / 18.0, 5.0 / 18.0]

    def bernstein(t):
        return [(1.0 - t) * (1.0 - t), 2.0 * t * (1.0 - t), t * t]

    def bern_slope(t):
        return [-2.0 * (1.0 - t), 2.0 - 4.0 * t, 2.0 * t]

    def lagrange(a, t):
        result = 1.0
        for m in range(3):
            if m != a:
                result = result * (t - points[m]) / (points[a] - points[m])
        return result

    def lagrange_slope(a, t):
        result = 0.0
        for k in range(3):
            if k != a:
                factor = 1.0 / (points[a] - points[k])
                for m in range(3):
                    if m != a and m != k:
                        factor = factor * (t - points[m]) / (points[a] - points[m])
                result = result + factor
        return result

    return {
        "eval_b": [[bernstein(points[q])[a] for q in range(3)] for a in range(3)],
        "force_b": [[weights[q] * bernstein(points[q])[a] for a in range(3)] for q in range(3)],
        "force_d": [[weights[q] * bern_slope(points[q])[a] for a in range(3)] for q in range(3)],
        "volume": [
            [weights[q] * lagrange_slope(a, points[q]) / weights[a] for a in range(3)]
            for q in range(3)
        ],
        "low_trace": [lagrange(a, 0.0) for a in range(3)],
        "high_trace": [lagrange(a, 1.0) for a in range(3)],
        "low_lift": [lagrange(a, 0.0) / weights[a] for a in range(3)],
        "high_lift": [lagrange(a, 1.0) / weights[a] for a in range(3)],
    }


TAB = tables()


def even_along(axes):
    return lax.rem(lax.axis_index(axes[-1]), 2) == 0


def row_index():
    return lax.broadcasted_iota(jnp.int32, TILE, 0)


def lane_index():
    return lax.broadcasted_iota(jnp.int32, TILE, 1)


def roll_rows(x, by):
    return pltpu.roll(x, by % 8, 0)


def roll_lanes(x, by):
    by = by % 128
    return x if by == 0 else pltpu.roll(x, by, 1)


class Shifts:
    def __init__(self):
        row = row_index()
        lane = lane_index()
        self.first = {2: (row & 2) == 0, 1: (row & 1) == 0}
        self.own = row < 4
        self.top = lane == 127
        self.bottom = lane == 0

    def pack_low(self, a, b, step):
        return a if b is None else jnp.where(self.first[step], a, roll_rows(b, step))

    def pack_high(self, a, b, step):
        return a if b is None else jnp.where(self.first[step], roll_rows(b, -step), a)

    def prev(self, own, packed, second, step):
        outside = packed if second else roll_rows(packed, -step)
        return jnp.where(self.first[step], outside, roll_rows(own, step))

    def next(self, own, packed, second, step):
        outside = packed if second else roll_rows(packed, step)
        return jnp.where(self.first[step], roll_rows(own, -step), outside)

    def beside(self, over, under, step):
        return jnp.where(self.first[step], over, under)

    def before(self, first_from, second_from, step):
        return jnp.where(
            self.first[step], roll_rows(first_from, -step), roll_rows(second_from, step)
        )

    def z_prev(self, x):
        t = roll_lanes(x, 1)
        return jnp.where(self.bottom, roll_rows(t, 4), t)

    def z_next(self, x):
        t = roll_lanes(x, -1)
        return jnp.where(self.top, roll_rows(t, 4), t)


def combine(values, coefs):
    total = None
    for value, coef in zip(values, coefs):
        if coef == 0.0:
            continue
        term = coef * value
        total = term if total is None else total + term
    return total


def column(matrix, j):
    return [matrix[i][j] for i in range(3)]


def contract(source, matrix, position):
    result = {}
    for key in source:
        if key[position] == 0:
            keys = [key[:position] + (m,) + key[position + 1 :] for m in range(3)]
            for j in range(3):
                result[keys[j]] = combine([source[k] for k in keys], column(matrix, j))
    return result


def message_size(*keys):
    tiles = -(-max(len(k) for k in keys) // 2)
    return -(-tiles // 2) + -(-tiles // 32)


def packed_tiles(sh, values, high, step):
    values = list(values)
    if len(values) % 2:
        values.append(None)
    pack = sh.pack_high if high else sh.pack_low
    tiles = [pack(values[n], values[n + 1], step) for n in range(0, len(values), 2)]
    group = lane_index() // 8
    halos = []
    for n, tile in enumerate(tiles):
        moved = roll_lanes(tile, 8 * (n % 16) + 4)
        if n % 16 == 0:
            halos.append(moved)
        else:
            halos[-1] = jnp.where(group == n % 16, moved, halos[-1])
    if len(tiles) % 2:
        tiles.append(tiles[-1])
    if len(halos) % 2:
        halos.append(halos[-1])
    return [
        jnp.where(sh.own, tiles[n], roll_rows(tiles[n + 1], 4)) for n in range(0, len(tiles), 2)
    ] + [jnp.where(sh.own, roll_rows(halos[n], 4), halos[n + 1]) for n in range(0, len(halos), 2)]


def write_messages(sh, even, near, far, over, under, step):
    over = packed_tiles(sh, over, True, step)
    under = packed_tiles(sh, under, False, step)
    for n in range(max(len(over), len(under))):
        up = over[min(n, len(over) - 1)]
        down = under[min(n, len(under) - 1)]
        near[n] = jnp.where(even, up, down)
        far[n] = jnp.where(even, down, up)


def read_messages(sh, even, near, far, over_keys, under_keys, step):
    def reader(first, second, keys, high):
        places = {key: n for n, key in enumerate(keys)}
        base = -(-(-(-len(keys) // 2)) // 2)
        packed = {}
        tiles = {}

        def load(k):
            if k not in packed:
                packed[k] = jnp.where(even, first[k], second[k])
            return packed[k]

        def get(key):
            n, odd = divmod(places[key], 2)
            if n not in tiles:
                main = load(n // 2)
                if n % 2:
                    main = roll_rows(main, 4)
                halo = load(base + n // 32)
                if n // 16 % 2 == 0:
                    halo = roll_rows(halo, 4)
                tiles[n] = jnp.where(sh.own, main, roll_lanes(halo, 124 - 8 * (n % 16)))
            if odd:
                return roll_rows(tiles[n], step if high else -step)
            return tiles[n]

        return get

    return reader(far, near, over_keys, True), reader(near, far, under_keys, False)


FIELDS = range(4)
TRIPLE = range(3)
PAIR = range(2)


def x_keys(high):
    keys = [("sum", f, a, b, z) for f in FIELDS for a in TRIPLE for b in TRIPLE for z in PAIR]
    nodes = 2 if high else 3
    keys += [("old", d, a, p, z) for d in TRIPLE for a in range(nodes) for p in PAIR for z in PAIR]
    return keys + side_keys()


def side_keys():
    keys = [("rho",) + key for key in POINTS]
    return keys + [("heat", m, n) for m in TRIPLE for n in TRIPLE]


def y_keys(high):
    keys = [("sum", f, a, b, z) for f in FIELDS for a in TRIPLE for b in TRIPLE for z in PAIR]
    keys += [("side", f, a, z) for f in FIELDS for a in TRIPLE for z in PAIR]
    nodes = 2 if high else 3
    keys += [("old", d, a, b, z) for d in TRIPLE for a in TRIPLE for b in range(nodes) for z in PAIR]
    if not high:
        keys += [("old_side", d, a, z) for d in TRIPLE for a in TRIPLE for z in PAIR]
    return keys + side_keys()


def side_values(rho, direction, trace):
    values = {("rho",) + key: rho[0, point(*key)] for key in POINTS}
    for m in TRIPLE:
        for n in TRIPLE:
            keys = [(a, m, n) if direction == 0 else (m, a, n) for a in TRIPLE]
            values["heat", m, n] = combine([rho[1, point(*k)] for k in keys], trace)
    return values


POINTS = [(a, b, c) for a in range(3) for b in range(3) for c in range(3)]


def point(a, b, c):
    return 9 * a + 3 * b + c


def pack_kernel(
    dens_far, ener_far, vel_far, near, far, both, nodes, top, dens, ener, vel, wide, split, sems
):
    lane = lane_index()
    even = even_along(GZ)
    copies = [
        pltpu.make_async_copy(source, target, sems.at[n])
        for n, (source, target) in enumerate(
            ((vel_far, vel), (ener_far, ener), (dens_far, dens))
        )
    ]
    for copy in copies:
        copy.start()
    copies[0].wait()
    half = (2 * lane) % 128
    for d in range(3):
        for px in range(2):
            slot = 2 * d + px
            wide[slot, 0:4, :] = vel[d, px]
            wide[slot, 4:8, :] = vel[d, 2 + px]
            left = wide[slot, :, 0:128]
            right = wide[slot, :, 128:256]
            for pz in range(2):
                picked = jnp.where(
                    lane < 64,
                    jnp.take_along_axis(left, half + pz, axis=1),
                    jnp.take_along_axis(right, half + pz, axis=1),
                )
                split[slot, 8 * pz : 8 * pz + 8, :] = picked
            for py in range(2):
                nodes[2 * slot + py] = split[slot, pl.ds(py, 8, stride=2), :]
    copies[1].wait()
    copies[2].wait()
    low = ener[0, 0]
    for q in range(27):
        for i in range(2):
            both[q, 2 * i : 2 * i + 2, :] = dens[q, i]
            both[q, 4 + 2 * i : 6 + 2 * i, :] = ener[q, i]
            low = jnp.maximum(low, ener[q, i])
    top[...] = jnp.broadcast_to(jnp.max(low, keepdims=True), top.shape)
    sources = [[both[q] for q in range(GROUP)], [both[q] for q in range(GROUP, 27)]]
    sources.append([nodes[n] for n in range(12)])
    for t in range(3):
        up = jnp.ones(TILE, F32)
        down = jnp.ones(TILE, F32)
        for g, tile in enumerate(sources[t]):
            group = lane // 4
            up = jnp.where(group == 2 * g, roll_lanes(tile, 8 * g - 124), up)
            down = jnp.where(group == 2 * g + 1, roll_lanes(tile, 8 * g + 4), down)
        near[t] = jnp.where(even, up, down)
        far[t] = jnp.where(even, down, up)


def top_kernel(tops, spread):
    spread[...] = jnp.broadcast_to(jnp.max(tops[...], axis=0, keepdims=True), spread.shape)


def step_kernel(tops, step):
    top = jnp.broadcast_to(jnp.max(tops[...], axis=0, keepdims=True), TILE)
    step[...] = CFL / jnp.sqrt((GAMMA * (GAMMA - 1.0)) * top)


def force_kernel(both, nodes, from_near, from_far, rho, vz, parts, near, far):
    sh = Shifts()
    below = ((lane_index() & 7) < 4) ^ (~even_along(GZ))
    merged = [jnp.where(below, from_far[t], from_near[t]) for t in range(3)]

    def extend(tile, t, g):
        halo = roll_lanes(merged[t], 124 - 8 * g)
        return (
            jnp.where(sh.own, tile, roll_rows(halo, 4)),
            jnp.where(sh.own, roll_rows(tile, 4), halo),
        )

    density = {}
    pressure = {}
    for key in POINTS:
        q = point(*key)
        dens, ener = extend(both[q], q // GROUP, q % GROUP)
        heat = dens * ener
        rho[0, q] = dens
        rho[1, q] = heat
        density[key] = dens
        pressure[key] = (GAMMA - 1.0) * heat
    for n in range(12):
        even, odd = extend(nodes[n], 2, n)
        vz[n, 0] = even
        vz[n, 1] = odd
    fb = TAB["force_b"]
    fd = TAB["force_d"]
    along_b = contract(pressure, fb, 0)
    along_d = contract(pressure, fd, 0)
    bb = contract(along_b, fb, 1)
    fields = [
        contract(contract(along_d, fb, 1), fb, 2),
        contract(contract(along_b, fd, 1), fb, 2),
        contract(bb, fd, 2),
        contract(contract(contract(density, fb, 0), fb, 1), fb, 2),
    ]
    for f in FIELDS:
        for a in TRIPLE:
            for b in TRIPLE:
                parts[f, 3 * a + b, 0] = fields[f][a, b, 0] + sh.z_prev(fields[f][a, b, 2])
                parts[f, 3 * a + b, 1] = fields[f][a, b, 1]
    lists = []
    for high, trace in ((True, "high_trace"), (False, "low_trace")):
        values = side_values(rho, 0, TAB[trace])
        for f in FIELDS:
            for b in TRIPLE:
                for z in PAIR:
                    line = [parts[f, 3 * a + b, z] for a in TRIPLE]
                    if high:
                        line[0] = line[0] + roll_rows(line[2], 2)
                    else:
                        line[2] = line[2] + roll_rows(line[0], -2)
                    for a in TRIPLE:
                        values["sum", f, a, b, z] = line[a]
        for d in TRIPLE:
            for p in PAIR:
                for z in PAIR:
                    first = vz[4 * d + p, z]
                    values["old", d, 0, p, z] = first
                    values["old", d, 1, p, z] = vz[4 * d + 2 + p, z]
                    values["old", d, 2, p, z] = roll_rows(first, -2)
        lists.append([values[key] for key in x_keys(high)])
    write_messages(sh, even_along(GX), near, far, *lists, 2)


def assemble(sh, own, side, step):
    inner = [own[0] + sh.before(side[2], own[2], step), own[1], own[2] + sh.before(own[0], side[0], step)]
    outer = [
        jnp.where(sh.first[step], side[0] + roll_rows(own[2], -step), side[0]),
        side[1],
        jnp.where(sh.first[step], side[2], side[2] + roll_rows(own[0], step)),
    ]
    return inner, outer


def rim_kernel(
    parts, vz, rho, from_near, from_far,
    sums, sums_x, old, old_x, rho_x, heat_x, near, far,
):
    sh = Shifts()
    left, right = read_messages(
        sh, even_along(GX), from_near, from_far, x_keys(True), x_keys(False), 2
    )

    def beside(*key):
        return sh.beside(right(key), left(key), 2)

    for f in FIELDS:
        for b in TRIPLE:
            for z in PAIR:
                own = [parts[f, 3 * a + b, z] for a in TRIPLE]
                side = [beside("sum", f, a, b, z) for a in TRIPLE]
                inner, outer = assemble(sh, own, side, 2)
                for a in TRIPLE:
                    sums[f, 3 * a + b, z] = inner[a]
                    sums_x[f, 3 * a + b, z] = outer[a]
    for d in TRIPLE:
        for p in PAIR:
            for z in PAIR:
                first = vz[4 * d + p, z]
                beyond = beside("old", d, 0, p, z)
                old[d, p, z] = first
                old[d, 2 + p, z] = vz[4 * d + 2 + p, z]
                old[d, 4 + p, z] = sh.before(first, beyond, 2)
                old_x[d, p, z] = beyond
                old_x[d, 2 + p, z] = beside("old", d, 1, p, z)
                old_x[d, 4 + p, z] = sh.beside(right(("old", d, 2, p, z)), roll_rows(first, 2), 2)
    for key in POINTS:
        rho_x[point(*key)] = beside("rho", *key)
    for m in TRIPLE:
        for n in TRIPLE:
            heat_x[3 * m + n] = beside("heat", m, n)
    lists = []
    for high, trace in ((True, "high_trace"), (False, "low_trace")):
        values = side_values(rho, 1, TAB[trace])
        for f in FIELDS:
            for a in TRIPLE:
                for z in PAIR:
                    line = [sums[f, 3 * a + b, z] for b in TRIPLE]
                    if high:
                        line[0] = line[0] + roll_rows(line[2], 1)
                    else:
                        line[2] = line[2] + roll_rows(line[0], -1)
                    for b in TRIPLE:
                        values["sum", f, a, b, z] = line[b]
                    values["side", f, a, z] = sums_x[f, 3 * a + (2 if high else 0), z]
        for d in TRIPLE:
            for a in TRIPLE:
                for z in PAIR:
                    first = old[d, 2 * a, z]
                    values["old", d, a, 0, z] = first
                    values["old", d, a, 1, z] = old[d, 2 * a + 1, z]
                    values["old", d, a, 2, z] = roll_rows(first, -1)
                    values["old_side", d, a, z] = old_x[d, 2 * a, z]
        lists.append([values[key] for key in y_keys(high)])
    write_messages(sh, even_along(GY), near, far, *lists, 1)


FACE_KEYS = [(f, m) for f in range(5) for m in range(9)]


def velocity_kernel(
    scale, sums, sums_x, old, old_x, rho, rho_x, heat_x, from_near, from_far,
    new_vel, u0, disp, speeds, sides, split, wide,
):
    sh = Shifts()
    lane = lane_index()
    step = scale[...]
    down, up = read_messages(
        sh, even_along(GY), from_near, from_far, y_keys(True), y_keys(False), 1
    )

    def beside(*key):
        return sh.beside(up(key), down(key), 1)

    centre = [{} for _ in TRIPLE]
    side_x = [{} for _ in TRIPLE]
    side_y = [{} for _ in TRIPLE]
    for a in TRIPLE:
        for z in PAIR:
            total = []
            for f in FIELDS:
                own = [sums[f, 3 * a + b, z] for b in TRIPLE]
                inner, outer = assemble(sh, own, [beside("sum", f, a, b, z) for b in TRIPLE], 1)
                aside = [sums_x[f, 3 * a + b, z] for b in TRIPLE]
                aside = [
                    aside[0] + sh.before(down(("side", f, a, z)), aside[2], 1),
                    aside[1],
                    aside[2] + sh.before(aside[0], up(("side", f, a, z)), 1),
                ]
                total.append((inner, aside, outer))
            for d in TRIPLE:
                first = old[d, 2 * a, z]
                first_x = old_x[d, 2 * a, z]
                beyond = beside("old", d, a, 0, z)
                olds = (
                    [first, old[d, 2 * a + 1, z], sh.before(first, beyond, 1)],
                    [
                        first_x,
                        old_x[d, 2 * a + 1, z],
                        sh.before(first_x, up(("old_side", d, a, z)), 1),
                    ],
                    [
                        beyond,
                        beside("old", d, a, 1, z),
                        sh.beside(up(("old", d, a, 2, z)), roll_rows(first, 1), 1),
                    ],
                )
                for kind, target in enumerate((centre, side_x, side_y)):
                    for b in TRIPLE:
                        over_mass = step / total[3][kind][b]
                        target[d][a, b, z] = olds[kind][b] + total[d][kind][b] * over_mass
    vel = centre
    for d in range(3):
        for px in range(2):
            slot = 2 * d + px
            for py in range(2):
                even = vel[d][px, py, 0]
                odd = vel[d][px, py, 1]
                tile = jnp.where(row_index() < 4, even, roll_rows(odd, 4))
                split[slot, pl.ds(py, 8, stride=2), :] = tile
            even = split[slot, 0:8, :]
            odd = split[slot, 8:16, :]
            for part in range(2):
                at = 64 * part + lane // 2
                wide[slot, :, 128 * part : 128 * part + 128] = jnp.where(
                    (lane & 1) == 0,
                    jnp.take_along_axis(even, at, axis=1),
                    jnp.take_along_axis(odd, at, axis=1),
                )
            new_vel[d, px] = wide[slot, 0:4, :]
            new_vel[d, 2 + px] = wide[slot, 4:8, :]
    eb = TAB["eval_b"]
    minus = -step

    def along_z(even, odd):
        line = [even, odd, sh.z_next(even)]
        return [combine(line, column(eb, q)) for q in range(3)]

    def at_points(nodes, own):
        gauss = [{} for _ in range(3)]
        for d in range(3):
            across = {}
            for b in range(3):
                for z in range(2):
                    line = [nodes[d][a, b, z] for a in range(3)]
                    for q in range(3):
                        across[q, b, z] = combine(line, column(eb, q))
            if d == 1 and own:
                for b, at in ((0, 2), (2, 3)):
                    for q in range(3):
                        for c, value in enumerate(along_z(across[q, b, 0], across[q, b, 1])):
                            speeds[at, 3 * q + c] = minus * value
            for qx in range(3):
                for qy in range(3):
                    pair = [
                        combine([across[qx, b, z] for b in range(3)], column(eb, qy))
                        for z in range(2)
                    ]
                    if d == 2 and own:
                        speeds[4, 3 * qx + qy] = minus * pair[0]
                    for c, value in enumerate(along_z(*pair)):
                        gauss[d][qx, qy, c] = value
                        if own:
                            disp[d, point(qx, qy, c)] = minus * value
        return gauss

    for a, at in ((0, 0), (2, 1)):
        for q in range(3):
            pair = [combine([vel[0][a, b, z] for b in range(3)], column(eb, q)) for z in range(2)]
            for c, value in enumerate(along_z(*pair)):
                speeds[at, 3 * q + c] = minus * value
    gauss = at_points(centre, True)
    for q in range(27):
        u0[0, q] = rho[0, q]
        u0[1, q] = rho[1, q]
    for d in range(3):
        for key in POINTS:
            u0[2 + d, point(*key)] = rho[0, point(*key)] * gauss[d][key]
    low = TAB["low_trace"]
    high = TAB["high_trace"]
    for side, nodes in enumerate((side_x, side_y)):
        turn = 2 - side
        gauss = at_points(nodes, False)
        trace = [jnp.where(sh.first[turn], low[a], high[a]) for a in TRIPLE]
        weigh = {}
        for key in POINTS:
            dens = beside("rho", *key) if side else rho_x[point(*key)]
            weigh[key] = trace[key[side]] * dens
        for m in TRIPLE:
            for n in TRIPLE:
                keys = [(a, m, n) if side == 0 else (m, a, n) for a in TRIPLE]
                at = 3 * m + n
                sides[side, 0, at] = weigh[keys[0]] + weigh[keys[1]] + weigh[keys[2]]
                sides[side, 1, at] = beside("heat", m, n) if side else heat_x[at]
                for d in TRIPLE:
                    sides[side, 2 + d, at] = sum(weigh[k] * gauss[d][k] for k in keys)


def stage_kernel(weight, last, *refs):
    refs = list(refs)
    u0 = refs.pop(0)
    u = u0 if weight is None else refs.pop(0)
    disp, speeds = refs[:2]
    sh = Shifts()
    even = [even_along(GX), even_along(GY)]
    if weight is None:
        sides = refs[2]
        outs = refs[3:]
    else:
        outs = refs[6:]
        sides = outs.pop()
        for d in range(2):
            step = 2 - d
            near, far = refs[2 + 2 * d : 4 + 2 * d]
            under, over = read_messages(sh, even[d], near, far, FACE_KEYS, FACE_KEYS, step)
            for f, m in FACE_KEYS:
                sides[d, f, m] = sh.beside(over((f, m)), under((f, m)), step)
    traces = None if last else outs.pop()
    low = TAB["low_trace"]
    high = TAB["high_trace"]
    low_lift = TAB["low_lift"]
    high_lift = TAB["high_lift"]
    volume = TAB["volume"]

    def one_field(f, carry):
        fields = {key: u[f, point(*key)] for key in POINTS}
        rate = {}
        for d in range(3):
            for m in range(3):
                for n in range(3):
                    if d == 0:
                        keys = [(a, m, n) for a in range(3)]
                    elif d == 1:
                        keys = [(m, a, n) for a in range(3)]
                    else:
                        keys = [(m, n, a) for a in range(3)]
                    at = 3 * m + n
                    line = [fields[k] for k in keys]
                    moved = [disp[d, point(*k)] * fields[k] for k in keys]
                    tm = combine(line, low)
                    tp = combine(line, high)
                    if d < 2:
                        step = 2 - d
                        before = sh.before(sides[d, f, at], tp, step)
                        after = sh.before(tm, sides[d, f, at], step)
                        s_low = speeds[2 * d, at]
                        s_high = speeds[2 * d + 1, at]
                        f_low = s_low * jnp.where(s_low > 0.0, before, tm)
                        f_high = s_high * jnp.where(s_high > 0.0, tp, after)
                    else:
                        s_low = speeds[4, at]
                        f_low = s_low * jnp.where(s_low > 0.0, sh.z_prev(tp), tm)
                        f_high = sh.z_next(f_low)
                    for a in range(3):
                        piece = combine(
                            moved + [f_low, f_high],
                            column(volume, a) + [low_lift[a], -high_lift[a]],
                        )
                        rate[keys[a]] = rate[keys[a]] + piece if d else piece
        after = {}
        for key in POINTS:
            q = point(*key)
            if weight is None:
                value = fields[key] + rate[key]
            else:
                value = (1.0 - weight) * u0[f, q] + weight * (fields[key] + rate[key])
            if last:
                outs[0][f, q, 0] = value[0:2]
                outs[0][f, q, 1] = value[2:4]
            else:
                outs[0][f, q] = value
                after[key] = value
        if not last:
            for d in range(2):
                for m in range(3):
                    for n in range(3):
                        keys = [(a, m, n) if d == 0 else (m, a, n) for a in range(3)]
                        line = [after[k] for k in keys]
                        traces[2 * d, f, 3 * m + n] = combine(line, high)
                        traces[2 * d + 1, f, 3 * m + n] = combine(line, low)
        return carry

    lax.fori_loop(0, 5, one_field, 0)
    if not last:
        for d in range(2):
            lists = [[traces[2 * d + k, f, m] for f, m in FACE_KEYS] for k in range(2)]
            write_messages(sh, even[d], outs[1 + 2 * d], outs[2 + 2 * d], *lists, 2 - d)


def call(kernel, outs, *args, scratch=(), name=None, weigh=None, far=False):
    space = pltpu.HBM if far else pltpu.VMEM
    return pl.pallas_call(
        kernel,
        out_shape=[jax.ShapeDtypeStruct(o, F32) for o in outs],
        in_specs=[pl.BlockSpec(memory_space=space) for _ in args],
        out_specs=[pl.BlockSpec(memory_space=pltpu.VMEM)] * len(outs),
        scratch_shapes=[pltpu.VMEM(s, F32) if isinstance(s, tuple) else s for s in scratch],
        compiler_params=pltpu.CompilerParams(vmem_limit_bytes=32 * 1024 * 1024),
        cost_estimate=weigh,
        name=name,
    )(*args)


def axis_count(axes):
    return math.prod(lax.axis_size(axis) for axis in axes)


def near_swap(value, axis):
    return lax.ppermute(value, axis, [(i, i ^ 1) for i in range(axis_count(axis))])


def far_swap(value, axis):
    count = axis_count(axis)
    return lax.ppermute(value, axis, [(i, (i + 2 * (i % 2) - 1) % count) for i in range(count)])


def exchange(near_x, far_x, near_y, far_y):
    far_y = far_swap(far_y, GY)
    far_x = far_swap(far_x, GX)
    near_x = near_swap(near_x, GX)
    near_y = near_swap(near_y, GY)
    return near_x, far_x, near_y, far_y


def shards(density, energy, velocity):
    tile = TILE
    dens = density.reshape((27,) + density.shape[3:])
    ener = energy.reshape((27,) + energy.shape[3:])
    near, far, both, nodes, top = call(
        pack_kernel,
        [(3,) + tile, (3,) + tile, (27,) + tile, (12,) + tile, (axis_count(FIRST), 128)],
        dens, ener, velocity,
        scratch=[
            dens.shape, ener.shape, velocity.shape,
            (6, 8, 256), (6, 16, 128), pltpu.SemaphoreType.DMA((3,)),
        ],
        far=True,
        name="pack",
    )
    far = far_swap(far, GZ)
    near = near_swap(near, GZ)
    tops = lax.all_to_all(top, FIRST, 0, 0, tiled=True)
    (top,) = call(top_kernel, [(axis_count(SECOND), 128)], tops, name="top", weigh=WEIGHT)
    tops = lax.all_to_all(top, SECOND, 0, 0, tiled=True)
    (step,) = call(step_kernel, [tile], tops, name="step", weigh=WEIGHT)
    parts_shape = (4, 9, 2) + tile
    old_shape = (3, 6, 2) + tile
    message = (message_size(x_keys(True), x_keys(False)),) + tile
    rho, vz, parts, near, far = call(
        force_kernel,
        [(2, 27) + tile, (12, 2) + tile, parts_shape, message, message],
        both, nodes, near, far,
        name="force",
    )
    far = far_swap(far, GX)
    near = near_swap(near, GX)
    message = (message_size(y_keys(True), y_keys(False)),) + tile
    sums, sums_x, old, old_x, rho_x, heat_x, near, far = call(
        rim_kernel,
        [
            parts_shape, parts_shape, old_shape, old_shape, (27,) + tile, (9,) + tile,
            message, message,
        ],
        parts, vz, rho, near, far,
        name="rim",
    )
    far = far_swap(far, GY)
    near = near_swap(near, GY)
    state = (5, 27) + tile
    new_velocity, u0, disp, speeds, sides = call(
        velocity_kernel,
        [velocity.shape, state, (3, 27) + tile, (5, 9) + tile, (2, 5, 9) + tile],
        step, sums, sums_x, old, old_x, rho, rho_x, heat_x, near, far,
        scratch=[(6, 16, 128), (6, 8, 256)],
        name="velocity",
    )
    faces = [(message_size(FACE_KEYS),) + tile] * 4
    held = (4, 5, 9) + tile
    one, *messages = call(
        functools.partial(stage_kernel, None, False), [state] + faces,
        u0, disp, speeds, sides,
        scratch=[held],
        name="stage_one",
    )
    two, *messages = call(
        functools.partial(stage_kernel, 0.25, False), [state] + faces,
        u0, one, disp, speeds, *exchange(*messages),
        scratch=[held, sides.shape],
        name="stage_two",
    )
    (remapped,) = call(
        functools.partial(stage_kernel, 2.0 / 3.0, True), [(5, 27) + density.shape[3:]],
        u0, two, disp, speeds, *exchange(*messages),
        scratch=[sides.shape],
        name="stage_three",
    )
    return new_velocity, remapped.reshape((5, 3, 3, 3) + density.shape[3:])


def solution(mesh):
    across, high, deep = (mesh.shape[axis] for axis in ("gx", "gy", "gz"))
    devices = mesh.devices.reshape(across, high // 2, 2, 2, deep // 2)
    return jax.shard_map(
        shards,
        mesh=Mesh(devices, GX + GY + GZ),
        in_specs=(
            P(None, None, None, GX, GY, GZ),
            P(None, None, None, GX, GY, GZ),
            P(None, GX, GY, GZ),
        ),
        out_specs=(P(None, GX, GY, GZ), P(None, None, None, None, GX, GY, GZ)),
        check_vma=False,
    )
```

```python
import functools
import math

import jax
import jax.numpy as jnp
from jax import lax
from jax.experimental import pallas as pl
from jax.experimental.pallas import tpu as pltpu
from jax.sharding import Mesh
from jax.sharding import PartitionSpec as P

GAMMA = 1.4
CFL = 0.1
F32 = jnp.float32
TILE = (8, 128)
GX = ("gx",)
GY = ("zl", "co")
GZ = ("zh", "xx")
FLAT = ("gx", "xx")
DEEP = ("zl", "co", "zh")
FIRST, SECOND = ("xx","co"), ("gx","zl","zh")
WEIGHT = pl.CostEstimate(flops=10**11, bytes_accessed=10**8, transcendentals=0)
GROUP = 14


def tables():
    root = math.sqrt(0.6)
    points = [0.5 - 0.5 * root, 0.5, 0.5 + 0.5 * root]
    weights = [5.0 / 18.0, 8.0 / 18.0, 5.0 / 18.0]

    def bernstein(t):
        return [(1.0 - t) * (1.0 - t), 2.0 * t * (1.0 - t), t * t]

    def bern_slope(t):
        return [-2.0 * (1.0 - t), 2.0 - 4.0 * t, 2.0 * t]

    def lagrange(a, t):
        result = 1.0
        for m in range(3):
            if m != a:
                result = result * (t - points[m]) / (points[a] - points[m])
        return result

    def lagrange_slope(a, t):
        result = 0.0
        for k in range(3):
            if k != a:
                factor = 1.0 / (points[a] - points[k])
                for m in range(3):
                    if m != a and m != k:
                        factor = factor * (t - points[m]) / (points[a] - points[m])
                result = result + factor
        return result

    return {
        "eval_b": [[bernstein(points[q])[a] for q in range(3)] for a in range(3)],
        "force_b": [[weights[q] * bernstein(points[q])[a] for a in range(3)] for q in range(3)],
        "force_d": [[weights[q] * bern_slope(points[q])[a] for a in range(3)] for q in range(3)],
        "volume": [
            [weights[q] * lagrange_slope(a, points[q]) / weights[a] for a in range(3)]
            for q in range(3)
        ],
        "low_trace": [lagrange(a, 0.0) for a in range(3)],
        "high_trace": [lagrange(a, 1.0) for a in range(3)],
        "low_lift": [lagrange(a, 0.0) / weights[a] for a in range(3)],
        "high_lift": [lagrange(a, 1.0) / weights[a] for a in range(3)],
    }


TAB = tables()


def even_along(axes):
    return lax.rem(lax.axis_index(axes[-1]), 2) == 0


def row_index():
    return lax.broadcasted_iota(jnp.int32, TILE, 0)


def lane_index():
    return lax.broadcasted_iota(jnp.int32, TILE, 1)


def roll_rows(x, by):
    return pltpu.roll(x, by % 8, 0)


def roll_lanes(x, by):
    by = by % 128
    return x if by == 0 else pltpu.roll(x, by, 1)


class Shifts:
    def __init__(self):
        row = row_index()
        lane = lane_index()
        self.first = {2: (row & 2) == 0, 1: (row & 1) == 0}
        self.own = row < 4
        self.top = lane == 127
        self.bottom = lane == 0

    def pack_low(self, a, b, step):
        return a if b is None else jnp.where(self.first[step], a, roll_rows(b, step))

    def pack_high(self, a, b, step):
        return a if b is None else jnp.where(self.first[step], roll_rows(b, -step), a)

    def prev(self, own, packed, second, step):
        outside = packed if second else roll_rows(packed, -step)
        return jnp.where(self.first[step], outside, roll_rows(own, step))

    def next(self, own, packed, second, step):
        outside = packed if second else roll_rows(packed, step)
        return jnp.where(self.first[step], roll_rows(own, -step), outside)

    def beside(self, over, under, step):
        return jnp.where(self.first[step], over, under)

    def before(self, first_from, second_from, step):
        return jnp.where(
            self.first[step], roll_rows(first_from, -step), roll_rows(second_from, step)
        )

    def z_prev(self, x):
        t = roll_lanes(x, 1)
        return jnp.where(self.bottom, roll_rows(t, 4), t)

    def z_next(self, x):
        t = roll_lanes(x, -1)
        return jnp.where(self.top, roll_rows(t, 4), t)


def combine(values, coefs):
    total = None
    for value, coef in zip(values, coefs):
        if coef == 0.0:
            continue
        term = coef * value
        total = term if total is None else total + term
    return total


def column(matrix, j):
    return [matrix[i][j] for i in range(3)]


def both_traces(line):
    low = TAB["low_trace"]
    middle = low[1] * line[1] + (0.5 * (low[0] + low[2])) * (line[0] + line[2])
    slope = (0.5 * (low[0] - low[2])) * (line[0] - line[2])
    return middle + slope, middle - slope


def contract(source, matrix, position):
    result = {}
    for key in source:
        if key[position] == 0:
            keys = [key[:position] + (m,) + key[position + 1 :] for m in range(3)]
            for j in range(3):
                result[keys[j]] = combine([source[k] for k in keys], column(matrix, j))
    return result


def message_size(*keys):
    tiles = -(-max(len(k) for k in keys) // 2)
    return -(-tiles // 2) + -(-tiles // 32)


def packed_tiles(sh, values, high, step):
    values = list(values)
    if len(values) % 2:
        values.append(None)
    pack = sh.pack_high if high else sh.pack_low
    tiles = [pack(values[n], values[n + 1], step) for n in range(0, len(values), 2)]
    group = lane_index() // 8
    halos = []
    for n, tile in enumerate(tiles):
        moved = roll_lanes(tile, 8 * (n % 16) + 4)
        if n % 16 == 0:
            halos.append(moved)
        else:
            halos[-1] = jnp.where(group == n % 16, moved, halos[-1])
    if len(tiles) % 2:
        tiles.append(tiles[-1])
    if len(halos) % 2:
        halos.append(halos[-1])
    return [
        jnp.where(sh.own, tiles[n], roll_rows(tiles[n + 1], 4)) for n in range(0, len(tiles), 2)
    ] + [jnp.where(sh.own, roll_rows(halos[n], 4), halos[n + 1]) for n in range(0, len(halos), 2)]


def write_messages(sh, even, near, far, over, under, step):
    over = packed_tiles(sh, over, True, step)
    under = packed_tiles(sh, under, False, step)
    for n in range(max(len(over), len(under))):
        up = over[min(n, len(over) - 1)]
        down = under[min(n, len(under) - 1)]
        near[n] = jnp.where(even, up, down)
        far[n] = jnp.where(even, down, up)


def read_messages(sh, even, near, far, over_keys, under_keys, step):
    def reader(first, second, keys, high):
        places = {key: n for n, key in enumerate(keys)}
        base = -(-(-(-len(keys) // 2)) // 2)
        packed = {}
        tiles = {}

        def load(k):
            if k not in packed:
                packed[k] = jnp.where(even, first[k], second[k])
            return packed[k]

        def get(key):
            n, odd = divmod(places[key], 2)
            if n not in tiles:
                main = load(n // 2)
                if n % 2:
                    main = roll_rows(main, 4)
                halo = load(base + n // 32)
                if n // 16 % 2 == 0:
                    halo = roll_rows(halo, 4)
                tiles[n] = jnp.where(sh.own, main, roll_lanes(halo, 124 - 8 * (n % 16)))
            if odd:
                return roll_rows(tiles[n], step if high else -step)
            return tiles[n]

        return get

    return reader(far, near, over_keys, True), reader(near, far, under_keys, False)


FIELDS = range(4)
TRIPLE = range(3)
PAIR = range(2)


def x_keys(high):
    keys = [("sum", f, a, b, z) for f in FIELDS for a in TRIPLE for b in TRIPLE for z in PAIR]
    nodes = 2 if high else 3
    keys += [("old", d, a, p, z) for d in TRIPLE for a in range(nodes) for p in PAIR for z in PAIR]
    return keys + side_keys()


def side_keys():
    keys = [("rho",) + key for key in POINTS]
    return keys + [("heat", m, n) for m in TRIPLE for n in TRIPLE]


def y_keys(high):
    keys = [("sum", f, a, b, z) for f in FIELDS for a in TRIPLE for b in TRIPLE for z in PAIR]
    keys += [("side", f, a, z) for f in FIELDS for a in TRIPLE for z in PAIR]
    nodes = 2 if high else 3
    keys += [("old", d, a, b, z) for d in TRIPLE for a in TRIPLE for b in range(nodes) for z in PAIR]
    if not high:
        keys += [("old_side", d, a, z) for d in TRIPLE for a in TRIPLE for z in PAIR]
    return keys + side_keys()


def side_values(rho, direction, trace):
    values = {("rho",) + key: rho[0, point(*key)] for key in POINTS}
    for m in TRIPLE:
        for n in TRIPLE:
            keys = [(a, m, n) if direction == 0 else (m, a, n) for a in TRIPLE]
            values["heat", m, n] = combine([rho[1, point(*k)] for k in keys], trace)
    return values


POINTS = [(a, b, c) for a in range(3) for b in range(3) for c in range(3)]


def point(a, b, c):
    return 9 * a + 3 * b + c


def arrange_nodes(vel, nodes, wide, split):
    lane = lane_index()
    half = (2 * lane) % 128
    for d in range(3):
        for px in range(2):
            slot = 2 * d + px
            wide[slot, 0:4, :] = vel[d, px]
            wide[slot, 4:8, :] = vel[d, 2 + px]
            left = wide[slot, :, 0:128]
            right = wide[slot, :, 128:256]
            for pz in range(2):
                picked = jnp.where(
                    lane < 64,
                    jnp.take_along_axis(left, half + pz, axis=1),
                    jnp.take_along_axis(right, half + pz, axis=1),
                )
                split[slot, 8 * pz : 8 * pz + 8, :] = picked
            for py in range(2):
                nodes[2 * slot + py] = split[slot, pl.ds(py, 8, stride=2), :]


def arrange_points(dens, ener, both):
    for q in range(27):
        for i in range(2):
            both[q, 2 * i : 2 * i + 2, :] = dens[q, i]
            both[q, 4 + 2 * i : 6 + 2 * i, :] = ener[q, i]


def pack_kernel(
    dens_far, ener_far, vel_far, near, far, top, dens, ener, vel, both, nodes, wide, split, sems
):
    even = even_along(GZ)
    copies = [
        pltpu.make_async_copy(source, target, sems.at[n])
        for n, (source, target) in enumerate(
            ((vel_far, vel), (ener_far, ener), (dens_far, dens))
        )
    ]
    for copy in copies:
        copy.start()
    copies[0].wait()
    arrange_nodes(vel, nodes, wide, split)
    copies[1].wait()
    high = jnp.max(ener[...], axis=(0, 1))
    top[...] = jnp.broadcast_to(jnp.max(high, keepdims=True), top.shape)
    copies[2].wait()
    arrange_points(dens, ener, both)
    group = lane_index() // 4
    sources = [[both[q] for q in range(GROUP)], [both[q] for q in range(GROUP, 27)]]
    sources.append([nodes[n] for n in range(12)])
    for t in range(3):
        up = jnp.ones(TILE, F32)
        down = jnp.ones(TILE, F32)
        for g, tile in enumerate(sources[t]):
            up = jnp.where(group == 2 * g, roll_lanes(tile, 8 * g - 124), up)
            down = jnp.where(group == 2 * g + 1, roll_lanes(tile, 8 * g + 4), down)
        near[t] = jnp.where(even, up, down)
        far[t] = jnp.where(even, down, up)


def top_kernel(tops, spread):
    spread[...] = jnp.broadcast_to(jnp.max(tops[...], axis=0, keepdims=True), spread.shape)


def step_kernel(tops, step):
    top = jnp.broadcast_to(jnp.max(tops[...], axis=0, keepdims=True), TILE)
    step[...] = CFL / jnp.sqrt((GAMMA * (GAMMA - 1.0)) * top)


def force_kernel(
    dens, ener, vel, from_near, from_far, rho, vz, parts, near, far, both, nodes, wide, split
):
    sh = Shifts()
    arrange_points(dens, ener, both)
    arrange_nodes(vel, nodes, wide, split)
    below = ((lane_index() & 7) < 4) ^ (~even_along(GZ))
    merged = [jnp.where(below, from_far[t], from_near[t]) for t in range(3)]

    def extend(tile, t, g):
        halo = roll_lanes(merged[t], 124 - 8 * g)
        return (
            jnp.where(sh.own, tile, roll_rows(halo, 4)),
            jnp.where(sh.own, roll_rows(tile, 4), halo),
        )

    density = {}
    pressure = {}
    for key in POINTS:
        q = point(*key)
        inside, warmth = extend(both[q], q // GROUP, q % GROUP)
        heat = inside * warmth
        rho[0, q] = inside
        rho[1, q] = heat
        density[key] = inside
        pressure[key] = (GAMMA - 1.0) * heat
    for n in range(12):
        even, odd = extend(nodes[n], 2, n)
        vz[n, 0] = even
        vz[n, 1] = odd
    fb = TAB["force_b"]
    fd = TAB["force_d"]
    along_b = contract(pressure, fb, 0)
    along_d = contract(pressure, fd, 0)
    bb = contract(along_b, fb, 1)
    fields = [
        contract(contract(along_d, fb, 1), fb, 2),
        contract(contract(along_b, fd, 1), fb, 2),
        contract(bb, fd, 2),
        contract(contract(contract(density, fb, 0), fb, 1), fb, 2),
    ]
    for f in FIELDS:
        for a in TRIPLE:
            for b in TRIPLE:
                parts[f, 3 * a + b, 0] = fields[f][a, b, 0] + sh.z_prev(fields[f][a, b, 2])
                parts[f, 3 * a + b, 1] = fields[f][a, b, 1]
    lists = []
    for high, trace in ((True, "high_trace"), (False, "low_trace")):
        values = side_values(rho, 0, TAB[trace])
        for f in FIELDS:
            for b in TRIPLE:
                for z in PAIR:
                    line = [parts[f, 3 * a + b, z] for a in TRIPLE]
                    if high:
                        line[0] = line[0] + roll_rows(line[2], 2)
                    else:
                        line[2] = line[2] + roll_rows(line[0], -2)
                    for a in TRIPLE:
                        values["sum", f, a, b, z] = line[a]
        for d in TRIPLE:
            for p in PAIR:
                for z in PAIR:
                    first = vz[4 * d + p, z]
                    values["old", d, 0, p, z] = first
                    values["old", d, 1, p, z] = vz[4 * d + 2 + p, z]
                    values["old", d, 2, p, z] = roll_rows(first, -2)
        lists.append([values[key] for key in x_keys(high)])
    write_messages(sh, even_along(GX), near, far, *lists, 2)


def assemble(sh, own, side, step):
    inner = [own[0] + sh.before(side[2], own[2], step), own[1], own[2] + sh.before(own[0], side[0], step)]
    outer = [
        jnp.where(sh.first[step], side[0] + roll_rows(own[2], -step), side[0]),
        side[1],
        jnp.where(sh.first[step], side[2], side[2] + roll_rows(own[0], step)),
    ]
    return inner, outer


def rim_kernel(
    parts, vz, rho, from_near, from_far,
    sums, sums_x, old, old_x, rho_x, heat_x, near, far,
):
    sh = Shifts()
    left, right = read_messages(
        sh, even_along(GX), from_near, from_far, x_keys(True), x_keys(False), 2
    )

    def beside(*key):
        return sh.beside(right(key), left(key), 2)

    for f in FIELDS:
        for b in TRIPLE:
            for z in PAIR:
                own = [parts[f, 3 * a + b, z] for a in TRIPLE]
                side = [beside("sum", f, a, b, z) for a in TRIPLE]
                inner, outer = assemble(sh, own, side, 2)
                for a in TRIPLE:
                    sums[f, 3 * a + b, z] = inner[a]
                    sums_x[f, 3 * a + b, z] = outer[a]
    for d in TRIPLE:
        for p in PAIR:
            for z in PAIR:
                first = vz[4 * d + p, z]
                beyond = beside("old", d, 0, p, z)
                old[d, p, z] = first
                old[d, 2 + p, z] = vz[4 * d + 2 + p, z]
                old[d, 4 + p, z] = sh.before(first, beyond, 2)
                old_x[d, p, z] = beyond
                old_x[d, 2 + p, z] = beside("old", d, 1, p, z)
                old_x[d, 4 + p, z] = sh.beside(right(("old", d, 2, p, z)), roll_rows(first, 2), 2)
    for key in POINTS:
        rho_x[point(*key)] = beside("rho", *key)
    for m in TRIPLE:
        for n in TRIPLE:
            heat_x[3 * m + n] = beside("heat", m, n)
    lists = []
    for high, trace in ((True, "high_trace"), (False, "low_trace")):
        values = side_values(rho, 1, TAB[trace])
        for f in FIELDS:
            for a in TRIPLE:
                for z in PAIR:
                    line = [sums[f, 3 * a + b, z] for b in TRIPLE]
                    if high:
                        line[0] = line[0] + roll_rows(line[2], 1)
                    else:
                        line[2] = line[2] + roll_rows(line[0], -1)
                    for b in TRIPLE:
                        values["sum", f, a, b, z] = line[b]
                    values["side", f, a, z] = sums_x[f, 3 * a + (2 if high else 0), z]
        for d in TRIPLE:
            for a in TRIPLE:
                for z in PAIR:
                    first = old[d, 2 * a, z]
                    values["old", d, a, 0, z] = first
                    values["old", d, a, 1, z] = old[d, 2 * a + 1, z]
                    values["old", d, a, 2, z] = roll_rows(first, -1)
                    values["old_side", d, a, z] = old_x[d, 2 * a, z]
        lists.append([values[key] for key in y_keys(high)])
    write_messages(sh, even_along(GY), near, far, *lists, 1)


FACE_KEYS = [(f, m) for f in range(5) for m in range(9)]


def velocity_kernel(
    scale, sums, sums_x, old, old_x, rho, rho_x, heat_x, from_near, from_far,
    stored, u0, disp, speeds, sides, split, wide, new_vel, sem,
):
    sh = Shifts()
    lane = lane_index()
    step = scale[...]
    down, up = read_messages(
        sh, even_along(GY), from_near, from_far, y_keys(True), y_keys(False), 1
    )

    def beside(*key):
        return sh.beside(up(key), down(key), 1)

    centre = [{} for _ in TRIPLE]
    side_x = [{} for _ in TRIPLE]
    side_y = [{} for _ in TRIPLE]
    for a in TRIPLE:
        for z in PAIR:
            total = []
            for f in FIELDS:
                own = [sums[f, 3 * a + b, z] for b in TRIPLE]
                inner, outer = assemble(sh, own, [beside("sum", f, a, b, z) for b in TRIPLE], 1)
                aside = [sums_x[f, 3 * a + b, z] for b in TRIPLE]
                aside = [
                    aside[0] + sh.before(down(("side", f, a, z)), aside[2], 1),
                    aside[1],
                    aside[2] + sh.before(aside[0], up(("side", f, a, z)), 1),
                ]
                total.append((inner, aside, outer))
            for d in TRIPLE:
                first = old[d, 2 * a, z]
                first_x = old_x[d, 2 * a, z]
                beyond = beside("old", d, a, 0, z)
                olds = (
                    [first, old[d, 2 * a + 1, z], sh.before(first, beyond, 1)],
                    [
                        first_x,
                        old_x[d, 2 * a + 1, z],
                        sh.before(first_x, up(("old_side", d, a, z)), 1),
                    ],
                    [
                        beyond,
                        beside("old", d, a, 1, z),
                        sh.beside(up(("old", d, a, 2, z)), roll_rows(first, 1), 1),
                    ],
                )
                for kind, target in enumerate((centre, side_x, side_y)):
                    for b in TRIPLE:
                        over_mass = step / total[3][kind][b]
                        target[d][a, b, z] = olds[kind][b] + total[d][kind][b] * over_mass
    vel = centre
    for d in range(3):
        for px in range(2):
            slot = 2 * d + px
            for py in range(2):
                even = vel[d][px, py, 0]
                odd = vel[d][px, py, 1]
                tile = jnp.where(row_index() < 4, even, roll_rows(odd, 4))
                split[slot, pl.ds(py, 8, stride=2), :] = tile
            even = split[slot, 0:8, :]
            odd = split[slot, 8:16, :]
            for part in range(2):
                at = 64 * part + lane // 2
                wide[slot, :, 128 * part : 128 * part + 128] = jnp.where(
                    (lane & 1) == 0,
                    jnp.take_along_axis(even, at, axis=1),
                    jnp.take_along_axis(odd, at, axis=1),
                )
            new_vel[d, px] = wide[slot, 0:4, :]
            new_vel[d, 2 + px] = wide[slot, 4:8, :]
    store = pltpu.make_async_copy(new_vel, stored, sem)
    store.start()
    eb = TAB["eval_b"]
    minus = -step

    def along_z(even, odd):
        line = [even, odd, sh.z_next(even)]
        return [combine(line, column(eb, q)) for q in range(3)]

    def at_points(nodes, own):
        gauss = [{} for _ in range(3)]
        for d in range(3):
            across = {}
            for b in range(3):
                for z in range(2):
                    line = [nodes[d][a, b, z] for a in range(3)]
                    for q in range(3):
                        across[q, b, z] = combine(line, column(eb, q))
            if d == 1 and own:
                for b, at in ((0, 2), (2, 3)):
                    for q in range(3):
                        for c, value in enumerate(along_z(across[q, b, 0], across[q, b, 1])):
                            speeds[at, 3 * q + c] = minus * value
            for qx in range(3):
                for qy in range(3):
                    pair = [
                        combine([across[qx, b, z] for b in range(3)], column(eb, qy))
                        for z in range(2)
                    ]
                    if d == 2 and own:
                        speeds[4, 3 * qx + qy] = minus * pair[0]
                    for c, value in enumerate(along_z(*pair)):
                        gauss[d][qx, qy, c] = value
                        if own:
                            disp[d, point(qx, qy, c)] = minus * value
        return gauss

    for a, at in ((0, 0), (2, 1)):
        for q in range(3):
            pair = [combine([vel[0][a, b, z] for b in range(3)], column(eb, q)) for z in range(2)]
            for c, value in enumerate(along_z(*pair)):
                speeds[at, 3 * q + c] = minus * value
    gauss = at_points(centre, True)
    for q in range(27):
        u0[0, q] = rho[0, q]
        u0[1, q] = rho[1, q]
    for d in range(3):
        for key in POINTS:
            u0[2 + d, point(*key)] = rho[0, point(*key)] * gauss[d][key]
    low = TAB["low_trace"]
    high = TAB["high_trace"]
    for side, nodes in enumerate((side_x, side_y)):
        turn = 2 - side
        gauss = at_points(nodes, False)
        trace = [jnp.where(sh.first[turn], low[a], high[a]) for a in TRIPLE]
        weigh = {}
        for key in POINTS:
            dens = beside("rho", *key) if side else rho_x[point(*key)]
            weigh[key] = trace[key[side]] * dens
        for m in TRIPLE:
            for n in TRIPLE:
                keys = [(a, m, n) if side == 0 else (m, a, n) for a in TRIPLE]
                at = 3 * m + n
                sides[side, 0, at] = weigh[keys[0]] + weigh[keys[1]] + weigh[keys[2]]
                sides[side, 1, at] = beside("heat", m, n) if side else heat_x[at]
                for d in TRIPLE:
                    sides[side, 2 + d, at] = sum(weigh[k] * gauss[d][k] for k in keys)
    store.wait()


def stage_kernel(weight, last, *refs):
    refs = list(refs)
    u0 = refs.pop(0)
    u = u0 if weight is None else refs.pop(0)
    disp, speeds = refs[:2]
    sh = Shifts()
    even = [even_along(GX), even_along(GY)]
    if weight is None:
        sides = refs[2]
        outs = refs[3:]
    else:
        outs = refs[6:]
        if last:
            sems = outs.pop()
            ready = outs.pop()
        sides = outs.pop()
        for d in range(2):
            step = 2 - d
            near, far = refs[2 + 2 * d : 4 + 2 * d]
            under, over = read_messages(sh, even[d], near, far, FACE_KEYS, FACE_KEYS, step)
            for f, m in FACE_KEYS:
                sides[d, f, m] = sh.beside(over((f, m)), under((f, m)), step)
    traces = None if last else outs.pop()
    lift = TAB["low_lift"]
    volume = TAB["volume"]
    odd_w = 0.5 * (volume[0][0] - volume[2][0])
    even_w = 0.5 * (volume[0][0] + volume[2][0])
    odd_f = 0.5 * (lift[0] + lift[2])
    even_f = 0.5 * (lift[0] - lift[2])

    def one_field(f, carry):
        fields = {key: u[f, point(*key)] for key in POINTS}
        rate = {}
        for d in range(3):
            for m in range(3):
                for n in range(3):
                    if d == 0:
                        keys = [(a, m, n) for a in range(3)]
                    elif d == 1:
                        keys = [(m, a, n) for a in range(3)]
                    else:
                        keys = [(m, n, a) for a in range(3)]
                    at = 3 * m + n
                    line = [fields[k] for k in keys]
                    moved = [disp[d, point(*k)] * fields[k] for k in keys]
                    tm, tp = both_traces(line)
                    if d < 2:
                        step = 2 - d
                        before = sh.before(sides[d, f, at], tp, step)
                        after = sh.before(tm, sides[d, f, at], step)
                        s_low = speeds[2 * d, at]
                        s_high = speeds[2 * d + 1, at]
                        f_low = s_low * jnp.where(s_low > 0.0, before, tm)
                        f_high = s_high * jnp.where(s_high > 0.0, tp, after)
                    else:
                        s_low = speeds[4, at]
                        f_low = s_low * jnp.where(s_low > 0.0, sh.z_prev(tp), tm)
                        f_high = sh.z_next(f_low)
                    across = moved[0] - moved[2]
                    jump = f_low - f_high
                    odd = odd_w * across + odd_f * jump
                    even_part = even_w * (moved[0] + moved[2]) + volume[1][0] * moved[1]
                    even_part = even_part + even_f * (f_low + f_high)
                    pieces = [
                        odd + even_part,
                        volume[0][1] * across + lift[1] * jump,
                        odd - even_part,
                    ]
                    for k, piece in zip(keys, pieces):
                        rate[k] = rate[k] + piece if d else piece
        after = {}
        for key in POINTS:
            q = point(*key)
            if weight is None:
                value = fields[key] + rate[key]
            else:
                value = (1.0 - weight) * u0[f, q] + weight * (fields[key] + rate[key])
            if last:
                ready[f, q, 0] = value[0:2]
                ready[f, q, 1] = value[2:4]
            else:
                outs[0][f, q] = value
                after[key] = value
        if last:
            pltpu.make_async_copy(ready.at[f], outs[0].at[f], sems.at[f]).start()
        else:
            for d in range(2):
                for m in range(3):
                    for n in range(3):
                        keys = [(a, m, n) if d == 0 else (m, a, n) for a in range(3)]
                        tm, tp = both_traces([after[k] for k in keys])
                        traces[2 * d, f, 3 * m + n] = tp
                        traces[2 * d + 1, f, 3 * m + n] = tm
        return carry

    lax.fori_loop(0, 5, one_field, 0, unroll=True)
    if last:
        for f in range(5):
            pltpu.make_async_copy(ready.at[f], outs[0].at[f], sems.at[f]).wait()
    else:
        for d in range(2):
            lists = [[traces[2 * d + k, f, m] for f, m in FACE_KEYS] for k in range(2)]
            write_messages(sh, even[d], outs[1 + 2 * d], outs[2 + 2 * d], *lists, 2 - d)


def call(kernel, outs, *args, scratch=(), name=None, weigh=None, far=False, stored=()):
    space = pltpu.HBM if far else pltpu.VMEM
    return pl.pallas_call(
        kernel,
        out_shape=[jax.ShapeDtypeStruct(o, F32) for o in outs],
        in_specs=[pl.BlockSpec(memory_space=space) for _ in args],
        out_specs=[
            pl.BlockSpec(memory_space=pltpu.HBM if n in stored else pltpu.VMEM)
            for n in range(len(outs))
        ],
        scratch_shapes=[pltpu.VMEM(s, F32) if isinstance(s, tuple) else s for s in scratch],
        compiler_params=pltpu.CompilerParams(vmem_limit_bytes=(60 if far else 32) * 1024 * 1024),
        cost_estimate=weigh,
        name=name,
    )(*args)


def axis_count(axes):
    return math.prod(lax.axis_size(axis) for axis in axes)


def near_swap(value, axis):
    return lax.ppermute(value, axis, [(i, i ^ 1) for i in range(axis_count(axis))])


def far_swap(value, axis):
    count = axis_count(axis)
    return lax.ppermute(value, axis, [(i, (i + 2 * (i % 2) - 1) % count) for i in range(count)])


def exchange(near_x, far_x, near_y, far_y):
    far_y = far_swap(far_y, GY)
    far_x = far_swap(far_x, GX)
    near_x = near_swap(near_x, GX)
    near_y = near_swap(near_y, GY)
    return near_x, far_x, near_y, far_y


def shards(density, energy, velocity):
    tile = TILE
    dens = density.reshape((27,) + density.shape[3:])
    ener = energy.reshape((27,) + energy.shape[3:])
    arranged = [(27,) + tile, (12,) + tile, (6, 8, 256), (6, 16, 128)]
    near, far, top = call(
        pack_kernel,
        [(3,) + tile, (3,) + tile, (axis_count(FIRST), 128)],
        dens, ener, velocity,
        scratch=[dens.shape, ener.shape, velocity.shape] + arranged + [pltpu.SemaphoreType.DMA((3,))],
        far=True,
        name="pack",
    )
    far = far_swap(far, GZ)
    near = near_swap(near, GZ)
    tops = lax.all_to_all(top, FIRST, 0, 0, tiled=True)
    (top,) = call(top_kernel, [(axis_count(SECOND), 128)], tops, name="top", weigh=WEIGHT)
    tops = lax.all_to_all(top, SECOND, 0, 0, tiled=True)
    (step,) = call(step_kernel, [tile], tops, name="step", weigh=WEIGHT)
    parts_shape = (4, 9, 2) + tile
    old_shape = (3, 6, 2) + tile
    message = (message_size(x_keys(True), x_keys(False)),) + tile
    rho, vz, parts, near, far = call(
        force_kernel,
        [(2, 27) + tile, (12, 2) + tile, parts_shape, message, message],
        dens, ener, velocity, near, far,
        scratch=arranged,
        name="force",
    )
    far = far_swap(far, GX)
    near = near_swap(near, GX)
    message = (message_size(y_keys(True), y_keys(False)),) + tile
    sums, sums_x, old, old_x, rho_x, heat_x, near, far = call(
        rim_kernel,
        [
            parts_shape, parts_shape, old_shape, old_shape, (27,) + tile, (9,) + tile,
            message, message,
        ],
        parts, vz, rho, near, far,
        name="rim",
    )
    far = far_swap(far, GY)
    near = near_swap(near, GY)
    state = (5, 27) + tile
    new_velocity, u0, disp, speeds, sides = call(
        velocity_kernel,
        [velocity.shape, state, (3, 27) + tile, (5, 9) + tile, (2, 5, 9) + tile],
        step, sums, sums_x, old, old_x, rho, rho_x, heat_x, near, far,
        scratch=[(6, 16, 128), (6, 8, 256), velocity.shape, pltpu.SemaphoreType.DMA],
        stored=(0,),
        name="velocity",
    )
    faces = [(message_size(FACE_KEYS),) + tile] * 4
    held = (4, 5, 9) + tile
    one, *messages = call(
        functools.partial(stage_kernel, None, False), [state] + faces,
        u0, disp, speeds, sides,
        scratch=[held],
        name="stage_one",
    )
    two, *messages = call(
        functools.partial(stage_kernel, 0.25, False), [state] + faces,
        u0, one, disp, speeds, *exchange(*messages),
        scratch=[held, sides.shape],
        name="stage_two",
    )
    (remapped,) = call(
        functools.partial(stage_kernel, 2.0 / 3.0, True), [(5, 27) + density.shape[3:]],
        u0, two, disp, speeds, *exchange(*messages),
        scratch=[sides.shape, (5, 27) + density.shape[3:], pltpu.SemaphoreType.DMA((5,))],
        stored=(0,),
        name="stage_three",
    )
    return new_velocity, remapped.reshape((5, 3, 3, 3) + density.shape[3:])


def solution(mesh):
    across, high, deep = (mesh.shape[axis] for axis in ("gx", "gy", "gz"))
    devices = mesh.devices.reshape(across, high // 2, 2, 2, deep // 2)
    return jax.shard_map(
        shards,
        mesh=Mesh(devices, GX + GY + GZ),
        in_specs=(
            P(None, None, None, GX, GY, GZ),
            P(None, None, None, GX, GY, GZ),
            P(None, GX, GY, GZ),
        ),
        out_specs=(P(None, GX, GY, GZ), P(None, None, None, None, GX, GY, GZ)),
        check_vma=False,
    )
```

```python
import functools
import math

import jax
import jax.numpy as jnp
from jax import lax
from jax.experimental import pallas as pl
from jax.experimental.pallas import tpu as pltpu
from jax.sharding import Mesh
from jax.sharding import PartitionSpec as P

GAMMA = 1.4
CFL = 0.1
F32 = jnp.float32
TILE = (8, 128)
GX = ("gx",)
GY = ("zl", "co")
GZ = ("zh", "xx")
FLAT = ("gx", "xx")
DEEP = ("zl", "co", "zh")
FIRST, SECOND = ("xx","co"), ("gx","zl","zh")
ORDER = [("far", 0), ("far", 1), ("near", 0), ("near", 1)]
WEIGHT = pl.CostEstimate(flops=10**11, bytes_accessed=10**8, transcendentals=0)
GROUP = 14


def tables():
    root = math.sqrt(0.6)
    points = [0.5 - 0.5 * root, 0.5, 0.5 + 0.5 * root]
    weights = [5.0 / 18.0, 8.0 / 18.0, 5.0 / 18.0]

    def bernstein(t):
        return [(1.0 - t) * (1.0 - t), 2.0 * t * (1.0 - t), t * t]

    def bern_slope(t):
        return [-2.0 * (1.0 - t), 2.0 - 4.0 * t, 2.0 * t]

    def lagrange(a, t):
        result = 1.0
        for m in range(3):
            if m != a:
                result = result * (t - points[m]) / (points[a] - points[m])
        return result

    def lagrange_slope(a, t):
        result = 0.0
        for k in range(3):
            if k != a:
                factor = 1.0 / (points[a] - points[k])
                for m in range(3):
                    if m != a and m != k:
                        factor = factor * (t - points[m]) / (points[a] - points[m])
                result = result + factor
        return result

    return {
        "eval_b": [[bernstein(points[q])[a] for q in range(3)] for a in range(3)],
        "force_b": [[weights[q] * bernstein(points[q])[a] for a in range(3)] for q in range(3)],
        "force_d": [[weights[q] * bern_slope(points[q])[a] for a in range(3)] for q in range(3)],
        "volume": [
            [weights[q] * lagrange_slope(a, points[q]) / weights[a] for a in range(3)]
            for q in range(3)
        ],
        "low_trace": [lagrange(a, 0.0) for a in range(3)],
        "high_trace": [lagrange(a, 1.0) for a in range(3)],
        "low_lift": [lagrange(a, 0.0) / weights[a] for a in range(3)],
        "high_lift": [lagrange(a, 1.0) / weights[a] for a in range(3)],
    }


TAB = tables()


def even_along(axes):
    return lax.rem(lax.axis_index(axes[-1]), 2) == 0


def row_index():
    return lax.broadcasted_iota(jnp.int32, TILE, 0)


def lane_index():
    return lax.broadcasted_iota(jnp.int32, TILE, 1)


def roll_rows(x, by):
    return pltpu.roll(x, by % 8, 0)


def roll_lanes(x, by):
    by = by % 128
    return x if by == 0 else pltpu.roll(x, by, 1)


class Shifts:
    def __init__(self):
        row = row_index()
        lane = lane_index()
        self.first = {2: (row & 2) == 0, 1: (row & 1) == 0}
        self.own = row < 4
        self.top = lane == 127
        self.bottom = lane == 0

    def pack_low(self, a, b, step):
        return a if b is None else jnp.where(self.first[step], a, roll_rows(b, step))

    def pack_high(self, a, b, step):
        return a if b is None else jnp.where(self.first[step], roll_rows(b, -step), a)

    def prev(self, own, packed, second, step):
        outside = packed if second else roll_rows(packed, -step)
        return jnp.where(self.first[step], outside, roll_rows(own, step))

    def next(self, own, packed, second, step):
        outside = packed if second else roll_rows(packed, step)
        return jnp.where(self.first[step], roll_rows(own, -step), outside)

    def beside(self, over, under, step):
        return jnp.where(self.first[step], over, under)

    def before(self, first_from, second_from, step):
        return jnp.where(
            self.first[step], roll_rows(first_from, -step), roll_rows(second_from, step)
        )

    def z_prev(self, x):
        t = roll_lanes(x, 1)
        return jnp.where(self.bottom, roll_rows(t, 4), t)

    def z_next(self, x):
        t = roll_lanes(x, -1)
        return jnp.where(self.top, roll_rows(t, 4), t)


def combine(values, coefs):
    total = None
    for value, coef in zip(values, coefs):
        if coef == 0.0:
            continue
        term = coef * value
        total = term if total is None else total + term
    return total


def column(matrix, j):
    return [matrix[i][j] for i in range(3)]


def both_traces(line):
    low = TAB["low_trace"]
    middle = low[1] * line[1] + (0.5 * (low[0] + low[2])) * (line[0] + line[2])
    slope = (0.5 * (low[0] - low[2])) * (line[0] - line[2])
    return middle + slope, middle - slope


def contract(source, matrix, position):
    result = {}
    for key in source:
        if key[position] == 0:
            keys = [key[:position] + (m,) + key[position + 1 :] for m in range(3)]
            for j in range(3):
                result[keys[j]] = combine([source[k] for k in keys], column(matrix, j))
    return result


def message_size(*keys):
    tiles = -(-max(len(k) for k in keys) // 2)
    return -(-tiles // 2) + -(-tiles // 32)


def packed_tiles(sh, values, high, step):
    values = list(values)
    if len(values) % 2:
        values.append(None)
    pack = sh.pack_high if high else sh.pack_low
    tiles = [pack(values[n], values[n + 1], step) for n in range(0, len(values), 2)]
    group = lane_index() // 8
    halos = []
    for n, tile in enumerate(tiles):
        moved = roll_lanes(tile, 8 * (n % 16) + 4)
        if n % 16 == 0:
            halos.append(moved)
        else:
            halos[-1] = jnp.where(group == n % 16, moved, halos[-1])
    if len(tiles) % 2:
        tiles.append(tiles[-1])
    if len(halos) % 2:
        halos.append(halos[-1])
    return [
        jnp.where(sh.own, tiles[n], roll_rows(tiles[n + 1], 4)) for n in range(0, len(tiles), 2)
    ] + [jnp.where(sh.own, roll_rows(halos[n], 4), halos[n + 1]) for n in range(0, len(halos), 2)]


def write_messages(sh, even, near, far, over, under, step):
    over = packed_tiles(sh, over, True, step)
    under = packed_tiles(sh, under, False, step)
    for n in range(max(len(over), len(under))):
        up = over[min(n, len(over) - 1)]
        down = under[min(n, len(under) - 1)]
        near[n] = jnp.where(even, up, down)
        far[n] = jnp.where(even, down, up)


def read_messages(sh, even, near, far, over_keys, under_keys, step):
    def reader(first, second, keys, high):
        places = {key: n for n, key in enumerate(keys)}
        base = -(-(-(-len(keys) // 2)) // 2)
        packed = {}
        tiles = {}

        def load(k):
            if k not in packed:
                packed[k] = jnp.where(even, first[k], second[k])
            return packed[k]

        def get(key):
            n, odd = divmod(places[key], 2)
            if n not in tiles:
                main = load(n // 2)
                if n % 2:
                    main = roll_rows(main, 4)
                halo = load(base + n // 32)
                if n // 16 % 2 == 0:
                    halo = roll_rows(halo, 4)
                tiles[n] = jnp.where(sh.own, main, roll_lanes(halo, 124 - 8 * (n % 16)))
            if odd:
                return roll_rows(tiles[n], step if high else -step)
            return tiles[n]

        return get

    return reader(far, near, over_keys, True), reader(near, far, under_keys, False)


FIELDS = range(4)
TRIPLE = range(3)
PAIR = range(2)


def x_keys(high):
    keys = [("sum", f, a, b, z) for f in FIELDS for a in TRIPLE for b in TRIPLE for z in PAIR]
    nodes = 2 if high else 3
    keys += [("old", d, a, p, z) for d in TRIPLE for a in range(nodes) for p in PAIR for z in PAIR]
    return keys + side_keys()


def side_keys():
    keys = [("rho",) + key for key in POINTS]
    return keys + [("heat", m, n) for m in TRIPLE for n in TRIPLE]


def y_keys(high):
    keys = [("sum", f, a, b, z) for f in FIELDS for a in TRIPLE for b in TRIPLE for z in PAIR]
    keys += [("side", f, a, z) for f in FIELDS for a in TRIPLE for z in PAIR]
    nodes = 2 if high else 3
    keys += [("old", d, a, b, z) for d in TRIPLE for a in TRIPLE for b in range(nodes) for z in PAIR]
    if not high:
        keys += [("old_side", d, a, z) for d in TRIPLE for a in TRIPLE for z in PAIR]
    return keys + side_keys()


def side_values(rho, direction, trace):
    values = {("rho",) + key: rho[0, point(*key)] for key in POINTS}
    for m in TRIPLE:
        for n in TRIPLE:
            keys = [(a, m, n) if direction == 0 else (m, a, n) for a in TRIPLE]
            values["heat", m, n] = combine([rho[1, point(*k)] for k in keys], trace)
    return values


POINTS = [(a, b, c) for a in range(3) for b in range(3) for c in range(3)]


def point(a, b, c):
    return 9 * a + 3 * b + c


def arrange_nodes(vel, nodes, wide, split):
    lane = lane_index()
    half = (2 * lane) % 128
    for d in range(3):
        for px in range(2):
            slot = 2 * d + px
            wide[slot, 0:4, :] = vel[d, px]
            wide[slot, 4:8, :] = vel[d, 2 + px]
            left = wide[slot, :, 0:128]
            right = wide[slot, :, 128:256]
            for pz in range(2):
                picked = jnp.where(
                    lane < 64,
                    jnp.take_along_axis(left, half + pz, axis=1),
                    jnp.take_along_axis(right, half + pz, axis=1),
                )
                split[slot, 8 * pz : 8 * pz + 8, :] = picked
            for py in range(2):
                nodes[2 * slot + py] = split[slot, pl.ds(py, 8, stride=2), :]


def arrange_points(dens, ener, both):
    for q in range(27):
        for i in range(2):
            both[q, 2 * i : 2 * i + 2, :] = dens[q, i]
            both[q, 4 + 2 * i : 6 + 2 * i, :] = ener[q, i]


def pack_kernel(
    dens_far, ener_far, vel_far, near, far, top, dens, ener, vel, both, nodes, wide, split, sems
):
    even = even_along(GZ)
    copies = [
        pltpu.make_async_copy(source, target, sems.at[n])
        for n, (source, target) in enumerate(
            ((vel_far, vel), (ener_far, ener), (dens_far, dens))
        )
    ]
    for copy in copies:
        copy.start()
    copies[0].wait()
    arrange_nodes(vel, nodes, wide, split)
    copies[1].wait()
    high = jnp.max(ener[...], axis=(0, 1))
    top[...] = jnp.broadcast_to(jnp.max(high, keepdims=True), top.shape)
    copies[2].wait()
    arrange_points(dens, ener, both)
    group = lane_index() // 4
    sources = [[both[q] for q in range(GROUP)], [both[q] for q in range(GROUP, 27)]]
    sources.append([nodes[n] for n in range(12)])
    for t in range(3):
        up = jnp.ones(TILE, F32)
        down = jnp.ones(TILE, F32)
        for g, tile in enumerate(sources[t]):
            up = jnp.where(group == 2 * g, roll_lanes(tile, 8 * g - 124), up)
            down = jnp.where(group == 2 * g + 1, roll_lanes(tile, 8 * g + 4), down)
        near[t] = jnp.where(even, up, down)
        far[t] = jnp.where(even, down, up)


def top_kernel(tops, spread):
    spread[...] = jnp.broadcast_to(jnp.max(tops[...], axis=0, keepdims=True), spread.shape)


def step_kernel(tops, step):
    top = jnp.broadcast_to(jnp.max(tops[...], axis=0, keepdims=True), TILE)
    step[...] = CFL / jnp.sqrt((GAMMA * (GAMMA - 1.0)) * top)


def force_kernel(
    dens, ener, vel, from_far, from_near, rho, vz, parts, near, far, both, nodes, wide, split
):
    sh = Shifts()
    arrange_points(dens, ener, both)
    arrange_nodes(vel, nodes, wide, split)
    below = ((lane_index() & 7) < 4) ^ (~even_along(GZ))
    merged = [jnp.where(below, from_far[t], from_near[t]) for t in range(3)]

    def extend(tile, t, g):
        halo = roll_lanes(merged[t], 124 - 8 * g)
        return (
            jnp.where(sh.own, tile, roll_rows(halo, 4)),
            jnp.where(sh.own, roll_rows(tile, 4), halo),
        )

    density = {}
    pressure = {}
    for key in POINTS:
        q = point(*key)
        inside, warmth = extend(both[q], q // GROUP, q % GROUP)
        heat = inside * warmth
        rho[0, q] = inside
        rho[1, q] = heat
        density[key] = inside
        pressure[key] = (GAMMA - 1.0) * heat
    for n in range(12):
        even, odd = extend(nodes[n], 2, n)
        vz[n, 0] = even
        vz[n, 1] = odd
    fb = TAB["force_b"]
    fd = TAB["force_d"]
    along_b = contract(pressure, fb, 0)
    along_d = contract(pressure, fd, 0)
    bb = contract(along_b, fb, 1)
    fields = [
        contract(contract(along_d, fb, 1), fb, 2),
        contract(contract(along_b, fd, 1), fb, 2),
        contract(bb, fd, 2),
        contract(contract(contract(density, fb, 0), fb, 1), fb, 2),
    ]
    for f in FIELDS:
        for a in TRIPLE:
            for b in TRIPLE:
                parts[f, 3 * a + b, 0] = fields[f][a, b, 0] + sh.z_prev(fields[f][a, b, 2])
                parts[f, 3 * a + b, 1] = fields[f][a, b, 1]
    lists = []
    for high, trace in ((True, "high_trace"), (False, "low_trace")):
        values = side_values(rho, 0, TAB[trace])
        for f in FIELDS:
            for b in TRIPLE:
                for z in PAIR:
                    line = [parts[f, 3 * a + b, z] for a in TRIPLE]
                    if high:
                        line[0] = line[0] + roll_rows(line[2], 2)
                    else:
                        line[2] = line[2] + roll_rows(line[0], -2)
                    for a in TRIPLE:
                        values["sum", f, a, b, z] = line[a]
        for d in TRIPLE:
            for p in PAIR:
                for z in PAIR:
                    first = vz[4 * d + p, z]
                    values["old", d, 0, p, z] = first
                    values["old", d, 1, p, z] = vz[4 * d + 2 + p, z]
                    values["old", d, 2, p, z] = roll_rows(first, -2)
        lists.append([values[key] for key in x_keys(high)])
    write_messages(sh, even_along(GX), near, far, *lists, 2)


def assemble(sh, own, side, step):
    inner = [own[0] + sh.before(side[2], own[2], step), own[1], own[2] + sh.before(own[0], side[0], step)]
    outer = [
        jnp.where(sh.first[step], side[0] + roll_rows(own[2], -step), side[0]),
        side[1],
        jnp.where(sh.first[step], side[2], side[2] + roll_rows(own[0], step)),
    ]
    return inner, outer


def rim_kernel(
    parts, vz, rho, from_far, from_near,
    sums, sums_x, old, old_x, rho_x, heat_x, near, far,
):
    sh = Shifts()
    left, right = read_messages(
        sh, even_along(GX), from_near, from_far, x_keys(True), x_keys(False), 2
    )

    def beside(*key):
        return sh.beside(right(key), left(key), 2)

    for f in FIELDS:
        for b in TRIPLE:
            for z in PAIR:
                own = [parts[f, 3 * a + b, z] for a in TRIPLE]
                side = [beside("sum", f, a, b, z) for a in TRIPLE]
                inner, outer = assemble(sh, own, side, 2)
                for a in TRIPLE:
                    sums[f, 3 * a + b, z] = inner[a]
                    sums_x[f, 3 * a + b, z] = outer[a]
    for d in TRIPLE:
        for p in PAIR:
            for z in PAIR:
                first = vz[4 * d + p, z]
                beyond = beside("old", d, 0, p, z)
                old[d, p, z] = first
                old[d, 2 + p, z] = vz[4 * d + 2 + p, z]
                old[d, 4 + p, z] = sh.before(first, beyond, 2)
                old_x[d, p, z] = beyond
                old_x[d, 2 + p, z] = beside("old", d, 1, p, z)
                old_x[d, 4 + p, z] = sh.beside(right(("old", d, 2, p, z)), roll_rows(first, 2), 2)
    for key in POINTS:
        rho_x[point(*key)] = beside("rho", *key)
    for m in TRIPLE:
        for n in TRIPLE:
            heat_x[3 * m + n] = beside("heat", m, n)
    lists = []
    for high, trace in ((True, "high_trace"), (False, "low_trace")):
        values = side_values(rho, 1, TAB[trace])
        for f in FIELDS:
            for a in TRIPLE:
                for z in PAIR:
                    line = [sums[f, 3 * a + b, z] for b in TRIPLE]
                    if high:
                        line[0] = line[0] + roll_rows(line[2], 1)
                    else:
                        line[2] = line[2] + roll_rows(line[0], -1)
                    for b in TRIPLE:
                        values["sum", f, a, b, z] = line[b]
                    values["side", f, a, z] = sums_x[f, 3 * a + (2 if high else 0), z]
        for d in TRIPLE:
            for a in TRIPLE:
                for z in PAIR:
                    first = old[d, 2 * a, z]
                    values["old", d, a, 0, z] = first
                    values["old", d, a, 1, z] = old[d, 2 * a + 1, z]
                    values["old", d, a, 2, z] = roll_rows(first, -1)
                    values["old_side", d, a, z] = old_x[d, 2 * a, z]
        lists.append([values[key] for key in y_keys(high)])
    write_messages(sh, even_along(GY), near, far, *lists, 1)


FACE_KEYS = [(f, m) for f in range(5) for m in range(9)]


def velocity_kernel(
    scale, sums, sums_x, old, old_x, rho, rho_x, heat_x, from_far, from_near,
    stored, u0, disp, speeds, sides, split, wide, new_vel, sem,
):
    sh = Shifts()
    lane = lane_index()
    step = scale[...]
    down, up = read_messages(
        sh, even_along(GY), from_near, from_far, y_keys(True), y_keys(False), 1
    )

    def beside(*key):
        return sh.beside(up(key), down(key), 1)

    centre = [{} for _ in TRIPLE]
    side_x = [{} for _ in TRIPLE]
    side_y = [{} for _ in TRIPLE]
    for a in TRIPLE:
        for z in PAIR:
            total = []
            for f in FIELDS:
                own = [sums[f, 3 * a + b, z] for b in TRIPLE]
                inner, outer = assemble(sh, own, [beside("sum", f, a, b, z) for b in TRIPLE], 1)
                aside = [sums_x[f, 3 * a + b, z] for b in TRIPLE]
                aside = [
                    aside[0] + sh.before(down(("side", f, a, z)), aside[2], 1),
                    aside[1],
                    aside[2] + sh.before(aside[0], up(("side", f, a, z)), 1),
                ]
                total.append((inner, aside, outer))
            for d in TRIPLE:
                first = old[d, 2 * a, z]
                first_x = old_x[d, 2 * a, z]
                beyond = beside("old", d, a, 0, z)
                olds = (
                    [first, old[d, 2 * a + 1, z], sh.before(first, beyond, 1)],
                    [
                        first_x,
                        old_x[d, 2 * a + 1, z],
                        sh.before(first_x, up(("old_side", d, a, z)), 1),
                    ],
                    [
                        beyond,
                        beside("old", d, a, 1, z),
                        sh.beside(up(("old", d, a, 2, z)), roll_rows(first, 1), 1),
                    ],
                )
                for kind, target in enumerate((centre, side_x, side_y)):
                    for b in TRIPLE:
                        over_mass = step / total[3][kind][b]
                        target[d][a, b, z] = olds[kind][b] + total[d][kind][b] * over_mass
    vel = centre
    for d in range(3):
        for px in range(2):
            slot = 2 * d + px
            for py in range(2):
                even = vel[d][px, py, 0]
                odd = vel[d][px, py, 1]
                tile = jnp.where(row_index() < 4, even, roll_rows(odd, 4))
                split[slot, pl.ds(py, 8, stride=2), :] = tile
            even = split[slot, 0:8, :]
            odd = split[slot, 8:16, :]
            for part in range(2):
                at = 64 * part + lane // 2
                wide[slot, :, 128 * part : 128 * part + 128] = jnp.where(
                    (lane & 1) == 0,
                    jnp.take_along_axis(even, at, axis=1),
                    jnp.take_along_axis(odd, at, axis=1),
                )
            new_vel[d, px] = wide[slot, 0:4, :]
            new_vel[d, 2 + px] = wide[slot, 4:8, :]
    store = pltpu.make_async_copy(new_vel, stored, sem)
    store.start()
    eb = TAB["eval_b"]
    minus = -step

    def along_z(even, odd):
        line = [even, odd, sh.z_next(even)]
        return [combine(line, column(eb, q)) for q in range(3)]

    def at_points(nodes, own):
        gauss = [{} for _ in range(3)]
        for d in range(3):
            across = {}
            for b in range(3):
                for z in range(2):
                    line = [nodes[d][a, b, z] for a in range(3)]
                    for q in range(3):
                        across[q, b, z] = combine(line, column(eb, q))
            if d == 1 and own:
                for b, at in ((0, 2), (2, 3)):
                    for q in range(3):
                        for c, value in enumerate(along_z(across[q, b, 0], across[q, b, 1])):
                            speeds[at, 3 * q + c] = minus * value
            for qx in range(3):
                for qy in range(3):
                    pair = [
                        combine([across[qx, b, z] for b in range(3)], column(eb, qy))
                        for z in range(2)
                    ]
                    if d == 2 and own:
                        speeds[4, 3 * qx + qy] = minus * pair[0]
                    for c, value in enumerate(along_z(*pair)):
                        gauss[d][qx, qy, c] = value
                        if own:
                            disp[d, point(qx, qy, c)] = minus * value
        return gauss

    for a, at in ((0, 0), (2, 1)):
        for q in range(3):
            pair = [combine([vel[0][a, b, z] for b in range(3)], column(eb, q)) for z in range(2)]
            for c, value in enumerate(along_z(*pair)):
                speeds[at, 3 * q + c] = minus * value
    gauss = at_points(centre, True)
    for q in range(27):
        u0[0, q] = rho[0, q]
        u0[1, q] = rho[1, q]
    for d in range(3):
        for key in POINTS:
            u0[2 + d, point(*key)] = rho[0, point(*key)] * gauss[d][key]
    low = TAB["low_trace"]
    high = TAB["high_trace"]
    for side, nodes in enumerate((side_x, side_y)):
        turn = 2 - side
        gauss = at_points(nodes, False)
        trace = [jnp.where(sh.first[turn], low[a], high[a]) for a in TRIPLE]
        weigh = {}
        for key in POINTS:
            dens = beside("rho", *key) if side else rho_x[point(*key)]
            weigh[key] = trace[key[side]] * dens
        for m in TRIPLE:
            for n in TRIPLE:
                keys = [(a, m, n) if side == 0 else (m, a, n) for a in TRIPLE]
                at = 3 * m + n
                sides[side, 0, at] = weigh[keys[0]] + weigh[keys[1]] + weigh[keys[2]]
                sides[side, 1, at] = beside("heat", m, n) if side else heat_x[at]
                for d in TRIPLE:
                    sides[side, 2 + d, at] = sum(weigh[k] * gauss[d][k] for k in keys)
    store.wait()


def stage_kernel(weight, last, *refs):
    refs = list(refs)
    u0 = refs.pop(0)
    u = u0 if weight is None else refs.pop(0)
    disp, speeds = refs[:2]
    sh = Shifts()
    even = [even_along(GX), even_along(GY)]
    if weight is None:
        sides = refs[2]
        outs = refs[3:]
    else:
        outs = refs[6:]
        if last:
            sems = outs.pop()
            ready = outs.pop()
        sides = outs.pop()
        for d in range(2):
            step = 2 - d
            near, far = (refs[2 + ORDER.index((k, d))] for k in ("near", "far"))
            under, over = read_messages(sh, even[d], near, far, FACE_KEYS, FACE_KEYS, step)
            for f, m in FACE_KEYS:
                sides[d, f, m] = sh.beside(over((f, m)), under((f, m)), step)
    traces = None if last else outs.pop()
    lift = TAB["low_lift"]
    volume = TAB["volume"]
    odd_w = 0.5 * (volume[0][0] - volume[2][0])
    even_w = 0.5 * (volume[0][0] + volume[2][0])
    odd_f = 0.5 * (lift[0] + lift[2])
    even_f = 0.5 * (lift[0] - lift[2])

    def one_field(f, carry):
        fields = {key: u[f, point(*key)] for key in POINTS}
        rate = {}
        for d in range(3):
            for m in range(3):
                for n in range(3):
                    if d == 0:
                        keys = [(a, m, n) for a in range(3)]
                    elif d == 1:
                        keys = [(m, a, n) for a in range(3)]
                    else:
                        keys = [(m, n, a) for a in range(3)]
                    at = 3 * m + n
                    line = [fields[k] for k in keys]
                    moved = [disp[d, point(*k)] * fields[k] for k in keys]
                    tm, tp = both_traces(line)
                    if d < 2:
                        step = 2 - d
                        before = sh.before(sides[d, f, at], tp, step)
                        after = sh.before(tm, sides[d, f, at], step)
                        s_low = speeds[2 * d, at]
                        s_high = speeds[2 * d + 1, at]
                        f_low = s_low * jnp.where(s_low > 0.0, before, tm)
                        f_high = s_high * jnp.where(s_high > 0.0, tp, after)
                    else:
                        s_low = speeds[4, at]
                        f_low = s_low * jnp.where(s_low > 0.0, sh.z_prev(tp), tm)
                        f_high = sh.z_next(f_low)
                    across = moved[0] - moved[2]
                    jump = f_low - f_high
                    odd = odd_w * across + odd_f * jump
                    even_part = even_w * (moved[0] + moved[2]) + volume[1][0] * moved[1]
                    even_part = even_part + even_f * (f_low + f_high)
                    pieces = [
                        odd + even_part,
                        volume[0][1] * across + lift[1] * jump,
                        odd - even_part,
                    ]
                    for k, piece in zip(keys, pieces):
                        rate[k] = rate[k] + piece if d else piece
        after = {}
        for key in POINTS:
            q = point(*key)
            if weight is None:
                value = fields[key] + rate[key]
            else:
                value = (1.0 - weight) * u0[f, q] + weight * (fields[key] + rate[key])
            if last:
                ready[f, q, 0] = value[0:2]
                ready[f, q, 1] = value[2:4]
            else:
                outs[0][f, q] = value
                after[key] = value
        if last:
            pltpu.make_async_copy(ready.at[f], outs[0].at[f], sems.at[f]).start()
        else:
            for d in range(2):
                for m in range(3):
                    for n in range(3):
                        keys = [(a, m, n) if d == 0 else (m, a, n) for a in range(3)]
                        tm, tp = both_traces([after[k] for k in keys])
                        traces[2 * d, f, 3 * m + n] = tp
                        traces[2 * d + 1, f, 3 * m + n] = tm
        return carry

    lax.fori_loop(0, 5, one_field, 0, unroll=True)
    if last:
        for f in range(5):
            pltpu.make_async_copy(ready.at[f], outs[0].at[f], sems.at[f]).wait()
    else:
        for d in range(2):
            lists = [[traces[2 * d + k, f, m] for f, m in FACE_KEYS] for k in range(2)]
            write_messages(sh, even[d], outs[1 + 2 * d], outs[2 + 2 * d], *lists, 2 - d)


def call(kernel, outs, *args, scratch=(), name=None, weigh=None, far=False, stored=()):
    space = pltpu.HBM if far else pltpu.VMEM
    return pl.pallas_call(
        kernel,
        out_shape=[jax.ShapeDtypeStruct(o, F32) for o in outs],
        in_specs=[pl.BlockSpec(memory_space=space) for _ in args],
        out_specs=[
            pl.BlockSpec(memory_space=pltpu.HBM if n in stored else pltpu.VMEM)
            for n in range(len(outs))
        ],
        scratch_shapes=[pltpu.VMEM(s, F32) if isinstance(s, tuple) else s for s in scratch],
        compiler_params=pltpu.CompilerParams(vmem_limit_bytes=(60 if far else 32) * 1024 * 1024),
        cost_estimate=weigh,
        name=name,
    )(*args)


def axis_count(axes):
    return math.prod(lax.axis_size(axis) for axis in axes)


def near_swap(value, axis):
    return lax.ppermute(value, axis, [(i, i ^ 1) for i in range(axis_count(axis))])


def far_swap(value, axis):
    count = axis_count(axis)
    return lax.ppermute(value, axis, [(i, (i + 2 * (i % 2) - 1) % count) for i in range(count)])


def exchange(near_x, far_x, near_y, far_y):
    received = {
        ("near", 0): near_swap(near_x, GX),
        ("far", 0): far_swap(far_x, GX),
        ("near", 1): near_swap(near_y, GY),
        ("far", 1): far_swap(far_y, GY),
    }
    return [received[key] for key in ORDER]


def shards(density, energy, velocity):
    tile = TILE
    dens = density.reshape((27,) + density.shape[3:])
    ener = energy.reshape((27,) + energy.shape[3:])
    arranged = [(27,) + tile, (12,) + tile, (6, 8, 256), (6, 16, 128)]
    near, far, top = call(
        pack_kernel,
        [(3,) + tile, (3,) + tile, (axis_count(FIRST), 128)],
        dens, ener, velocity,
        scratch=[dens.shape, ener.shape, velocity.shape] + arranged + [pltpu.SemaphoreType.DMA((3,))],
        far=True,
        name="pack",
    )
    far = far_swap(far, GZ)
    near = near_swap(near, GZ)
    tops = lax.all_to_all(top, FIRST, 0, 0, tiled=True)
    (top,) = call(top_kernel, [(axis_count(SECOND), 128)], tops, name="top", weigh=WEIGHT)
    tops = lax.all_to_all(top, SECOND, 0, 0, tiled=True)
    (step,) = call(step_kernel, [tile], tops, name="step", weigh=WEIGHT)
    parts_shape = (4, 9, 2) + tile
    old_shape = (3, 6, 2) + tile
    message = (message_size(x_keys(True), x_keys(False)),) + tile
    rho, vz, parts, near, far = call(
        force_kernel,
        [(2, 27) + tile, (12, 2) + tile, parts_shape, message, message],
        dens, ener, velocity, far, near,
        scratch=arranged,
        name="force",
    )
    far = far_swap(far, GX)
    near = near_swap(near, GX)
    message = (message_size(y_keys(True), y_keys(False)),) + tile
    sums, sums_x, old, old_x, rho_x, heat_x, near, far = call(
        rim_kernel,
        [
            parts_shape, parts_shape, old_shape, old_shape, (27,) + tile, (9,) + tile,
            message, message,
        ],
        parts, vz, rho, far, near,
        name="rim",
    )
    far = far_swap(far, GY)
    near = near_swap(near, GY)
    state = (5, 27) + tile
    new_velocity, u0, disp, speeds, sides = call(
        velocity_kernel,
        [velocity.shape, state, (3, 27) + tile, (5, 9) + tile, (2, 5, 9) + tile],
        step, sums, sums_x, old, old_x, rho, rho_x, heat_x, far, near,
        scratch=[(6, 16, 128), (6, 8, 256), velocity.shape, pltpu.SemaphoreType.DMA],
        stored=(0,),
        name="velocity",
    )
    faces = [(message_size(FACE_KEYS),) + tile] * 4
    held = (4, 5, 9) + tile
    one, *messages = call(
        functools.partial(stage_kernel, None, False), [state] + faces,
        u0, disp, speeds, sides,
        scratch=[held],
        name="stage_one",
    )
    two, *messages = call(
        functools.partial(stage_kernel, 0.25, False), [state] + faces,
        u0, one, disp, speeds, *exchange(*messages),
        scratch=[held, sides.shape],
        name="stage_two",
    )
    (remapped,) = call(
        functools.partial(stage_kernel, 2.0 / 3.0, True), [(5, 27) + density.shape[3:]],
        u0, two, disp, speeds, *exchange(*messages),
        scratch=[sides.shape, (5, 27) + density.shape[3:], pltpu.SemaphoreType.DMA((5,))],
        stored=(0,),
        name="stage_three",
    )
    return new_velocity, remapped.reshape((5, 3, 3, 3) + density.shape[3:])


def solution(mesh):
    across, high, deep = (mesh.shape[axis] for axis in ("gx", "gy", "gz"))
    devices = mesh.devices.reshape(across, high // 2, 2, 2, deep // 2)
    return jax.shard_map(
        shards,
        mesh=Mesh(devices, GX + GY + GZ),
        in_specs=(
            P(None, None, None, GX, GY, GZ),
            P(None, None, None, GX, GY, GZ),
            P(None, GX, GY, GZ),
        ),
        out_specs=(P(None, GX, GY, GZ), P(None, None, None, None, GX, GY, GZ)),
        check_vma=False,
    )
```

```python
import functools
import math

import jax
import jax.numpy as jnp
from jax import lax
from jax.experimental import pallas as pl
from jax.experimental.pallas import tpu as pltpu
from jax.sharding import Mesh
from jax.sharding import PartitionSpec as P

GAMMA = 1.4
CFL = 0.1
F32 = jnp.float32
TILE = (8, 128)
GX = ("gx",)
GY = ("zl", "co")
GZ = ("zh", "xx")
FLAT = ("gx", "xx")
DEEP = ("zl", "co", "zh")
FIRST, SECOND = ("xx","co"), ("gx","zl","zh")
ORDER = [("far", 0), ("far", 1), ("near", 0), ("near", 1)]
WEIGHT = pl.CostEstimate(flops=10**11, bytes_accessed=10**8, transcendentals=0)
GROUP = 14


def tables():
    root = math.sqrt(0.6)
    points = [0.5 - 0.5 * root, 0.5, 0.5 + 0.5 * root]
    weights = [5.0 / 18.0, 8.0 / 18.0, 5.0 / 18.0]

    def bernstein(t):
        return [(1.0 - t) * (1.0 - t), 2.0 * t * (1.0 - t), t * t]

    def bern_slope(t):
        return [-2.0 * (1.0 - t), 2.0 - 4.0 * t, 2.0 * t]

    def lagrange(a, t):
        result = 1.0
        for m in range(3):
            if m != a:
                result = result * (t - points[m]) / (points[a] - points[m])
        return result

    def lagrange_slope(a, t):
        result = 0.0
        for k in range(3):
            if k != a:
                factor = 1.0 / (points[a] - points[k])
                for m in range(3):
                    if m != a and m != k:
                        factor = factor * (t - points[m]) / (points[a] - points[m])
                result = result + factor
        return result

    return {
        "eval_b": [[bernstein(points[q])[a] for q in range(3)] for a in range(3)],
        "force_b": [[weights[q] * bernstein(points[q])[a] for a in range(3)] for q in range(3)],
        "force_d": [[weights[q] * bern_slope(points[q])[a] for a in range(3)] for q in range(3)],
        "volume": [
            [weights[q] * lagrange_slope(a, points[q]) / weights[a] for a in range(3)]
            for q in range(3)
        ],
        "low_trace": [lagrange(a, 0.0) for a in range(3)],
        "high_trace": [lagrange(a, 1.0) for a in range(3)],
        "low_lift": [lagrange(a, 0.0) / weights[a] for a in range(3)],
        "high_lift": [lagrange(a, 1.0) / weights[a] for a in range(3)],
    }


TAB = tables()


def even_along(axes):
    return lax.rem(lax.axis_index(axes[-1]), 2) == 0


def row_index():
    return lax.broadcasted_iota(jnp.int32, TILE, 0)


def lane_index():
    return lax.broadcasted_iota(jnp.int32, TILE, 1)


def roll_rows(x, by):
    return pltpu.roll(x, by % 8, 0)


def roll_lanes(x, by):
    by = by % 128
    return x if by == 0 else pltpu.roll(x, by, 1)


class Shifts:
    def __init__(self):
        row = row_index()
        lane = lane_index()
        self.first = {2: (row & 2) == 0, 1: (row & 1) == 0}
        self.own = row < 4
        self.top = lane == 127
        self.bottom = lane == 0

    def pack_low(self, a, b, step):
        return a if b is None else jnp.where(self.first[step], a, roll_rows(b, step))

    def pack_high(self, a, b, step):
        return a if b is None else jnp.where(self.first[step], roll_rows(b, -step), a)

    def prev(self, own, packed, second, step):
        outside = packed if second else roll_rows(packed, -step)
        return jnp.where(self.first[step], outside, roll_rows(own, step))

    def next(self, own, packed, second, step):
        outside = packed if second else roll_rows(packed, step)
        return jnp.where(self.first[step], roll_rows(own, -step), outside)

    def beside(self, over, under, step):
        return jnp.where(self.first[step], over, under)

    def before(self, first_from, second_from, step):
        return jnp.where(
            self.first[step], roll_rows(first_from, -step), roll_rows(second_from, step)
        )

    def z_prev(self, x):
        t = roll_lanes(x, 1)
        return jnp.where(self.bottom, roll_rows(t, 4), t)

    def z_next(self, x):
        t = roll_lanes(x, -1)
        return jnp.where(self.top, roll_rows(t, 4), t)


def combine(values, coefs):
    total = None
    for value, coef in zip(values, coefs):
        if coef == 0.0:
            continue
        term = coef * value
        total = term if total is None else total + term
    return total


def column(matrix, j):
    return [matrix[i][j] for i in range(3)]


def both_traces(line):
    low = TAB["low_trace"]
    middle = low[1] * line[1] + (0.5 * (low[0] + low[2])) * (line[0] + line[2])
    slope = (0.5 * (low[0] - low[2])) * (line[0] - line[2])
    return middle + slope, middle - slope


def contract(source, matrix, position):
    result = {}
    for key in source:
        if key[position] == 0:
            keys = [key[:position] + (m,) + key[position + 1 :] for m in range(3)]
            for j in range(3):
                result[keys[j]] = combine([source[k] for k in keys], column(matrix, j))
    return result


def message_size(*keys):
    tiles = -(-max(len(k) for k in keys) // 2)
    return -(-tiles // 2) + -(-tiles // 32)


def packed_tiles(sh, values, high, step):
    values = list(values)
    if len(values) % 2:
        values.append(None)
    pack = sh.pack_high if high else sh.pack_low
    tiles = [pack(values[n], values[n + 1], step) for n in range(0, len(values), 2)]
    group = lane_index() // 8
    halos = []
    for n, tile in enumerate(tiles):
        moved = roll_lanes(tile, 8 * (n % 16) + 4)
        if n % 16 == 0:
            halos.append(moved)
        else:
            halos[-1] = jnp.where(group == n % 16, moved, halos[-1])
    if len(tiles) % 2:
        tiles.append(tiles[-1])
    if len(halos) % 2:
        halos.append(halos[-1])
    return [
        jnp.where(sh.own, tiles[n], roll_rows(tiles[n + 1], 4)) for n in range(0, len(tiles), 2)
    ] + [jnp.where(sh.own, roll_rows(halos[n], 4), halos[n + 1]) for n in range(0, len(halos), 2)]


def write_messages(sh, even, near, far, over, under, step):
    over = packed_tiles(sh, over, True, step)
    under = packed_tiles(sh, under, False, step)
    for n in range(max(len(over), len(under))):
        up = over[min(n, len(over) - 1)]
        down = under[min(n, len(under) - 1)]
        near[n] = jnp.where(even, up, down)
        far[n] = jnp.where(even, down, up)


def read_messages(sh, even, near, far, over_keys, under_keys, step):
    def reader(first, second, keys, high):
        places = {key: n for n, key in enumerate(keys)}
        base = -(-(-(-len(keys) // 2)) // 2)
        packed = {}
        tiles = {}

        def load(k):
            if k not in packed:
                packed[k] = jnp.where(even, first[k], second[k])
            return packed[k]

        def get(key):
            n, odd = divmod(places[key], 2)
            if n not in tiles:
                main = load(n // 2)
                if n % 2:
                    main = roll_rows(main, 4)
                halo = load(base + n // 32)
                if n // 16 % 2 == 0:
                    halo = roll_rows(halo, 4)
                tiles[n] = jnp.where(sh.own, main, roll_lanes(halo, 124 - 8 * (n % 16)))
            if odd:
                return roll_rows(tiles[n], step if high else -step)
            return tiles[n]

        return get

    return reader(far, near, over_keys, True), reader(near, far, under_keys, False)


FIELDS = range(4)
TRIPLE = range(3)
PAIR = range(2)


def x_keys(high):
    keys = [("sum", f, a, b, z) for f in FIELDS for a in TRIPLE for b in TRIPLE for z in PAIR]
    nodes = 2 if high else 3
    keys += [("old", d, a, p, z) for d in TRIPLE for a in range(nodes) for p in PAIR for z in PAIR]
    return keys + side_keys()


def side_keys():
    keys = [("rho",) + key for key in POINTS]
    return keys + [("heat", m, n) for m in TRIPLE for n in TRIPLE]


def y_keys(high):
    keys = [("sum", f, a, b, z) for f in FIELDS for a in TRIPLE for b in TRIPLE for z in PAIR]
    keys += [("side", f, a, z) for f in FIELDS for a in ("mid", "far") for z in PAIR]
    nodes = 2 if high else 3
    keys += [("old", d, a, b, z) for d in TRIPLE for a in TRIPLE for b in range(nodes) for z in PAIR]
    if not high:
        keys += [("old_side", d, a, z) for d in TRIPLE for a in ("mid", "far") for z in PAIR]
    return keys + side_keys()


def side_values(rho, direction, trace):
    values = {("rho",) + key: rho[0, point(*key)] for key in POINTS}
    for m in TRIPLE:
        for n in TRIPLE:
            keys = [(a, m, n) if direction == 0 else (m, a, n) for a in TRIPLE]
            values["heat", m, n] = combine([rho[1, point(*k)] for k in keys], trace)
    return values


POINTS = [(a, b, c) for a in range(3) for b in range(3) for c in range(3)]


def point(a, b, c):
    return 9 * a + 3 * b + c


def arrange_nodes(vel, nodes, wide, split):
    lane = lane_index()
    half = (2 * lane) % 128
    for d in range(3):
        for px in range(2):
            slot = 2 * d + px
            wide[slot, 0:4, :] = vel[d, px]
            wide[slot, 4:8, :] = vel[d, 2 + px]
            left = wide[slot, :, 0:128]
            right = wide[slot, :, 128:256]
            for pz in range(2):
                picked = jnp.where(
                    lane < 64,
                    jnp.take_along_axis(left, half + pz, axis=1),
                    jnp.take_along_axis(right, half + pz, axis=1),
                )
                split[slot, 8 * pz : 8 * pz + 8, :] = picked
            for py in range(2):
                nodes[2 * slot + py] = split[slot, pl.ds(py, 8, stride=2), :]


def arrange_points(dens, ener, both):
    for q in range(27):
        for i in range(2):
            both[q, 2 * i : 2 * i + 2, :] = dens[q, i]
            both[q, 4 + 2 * i : 6 + 2 * i, :] = ener[q, i]


def pack_kernel(
    dens_far, ener_far, vel_far, near, far, top, dens, ener, vel, both, nodes, wide, split, sems
):
    even = even_along(GZ)
    copies = [
        pltpu.make_async_copy(source, target, sems.at[n])
        for n, (source, target) in enumerate(
            ((vel_far, vel), (ener_far, ener), (dens_far, dens))
        )
    ]
    for copy in copies:
        copy.start()
    copies[0].wait()
    arrange_nodes(vel, nodes, wide, split)
    copies[1].wait()
    high = jnp.max(ener[...], axis=(0, 1))
    top[...] = jnp.broadcast_to(jnp.max(high, keepdims=True), top.shape)
    copies[2].wait()
    arrange_points(dens, ener, both)
    group = lane_index() // 4
    sources = [[both[q] for q in range(GROUP)], [both[q] for q in range(GROUP, 27)]]
    sources.append([nodes[n] for n in range(12)])
    for t in range(3):
        up = jnp.ones(TILE, F32)
        down = jnp.ones(TILE, F32)
        for g, tile in enumerate(sources[t]):
            up = jnp.where(group == 2 * g, roll_lanes(tile, 8 * g - 124), up)
            down = jnp.where(group == 2 * g + 1, roll_lanes(tile, 8 * g + 4), down)
        near[t] = jnp.where(even, up, down)
        far[t] = jnp.where(even, down, up)


def top_kernel(tops, spread):
    spread[...] = jnp.broadcast_to(jnp.max(tops[...], axis=0, keepdims=True), spread.shape)


def step_kernel(tops, step):
    top = jnp.broadcast_to(jnp.max(tops[...], axis=0, keepdims=True), TILE)
    step[...] = CFL / jnp.sqrt((GAMMA * (GAMMA - 1.0)) * top)


def force_kernel(
    dens, ener, vel, from_far, from_near, rho, vz, parts, near, far, both, nodes, wide, split
):
    sh = Shifts()
    arrange_points(dens, ener, both)
    arrange_nodes(vel, nodes, wide, split)
    below = ((lane_index() & 7) < 4) ^ (~even_along(GZ))
    merged = [jnp.where(below, from_far[t], from_near[t]) for t in range(3)]

    def extend(tile, t, g):
        halo = roll_lanes(merged[t], 124 - 8 * g)
        return (
            jnp.where(sh.own, tile, roll_rows(halo, 4)),
            jnp.where(sh.own, roll_rows(tile, 4), halo),
        )

    density = {}
    pressure = {}
    for key in POINTS:
        q = point(*key)
        inside, warmth = extend(both[q], q // GROUP, q % GROUP)
        heat = inside * warmth
        rho[0, q] = inside
        rho[1, q] = heat
        density[key] = inside
        pressure[key] = (GAMMA - 1.0) * heat
    for n in range(12):
        even, odd = extend(nodes[n], 2, n)
        vz[n, 0] = even
        vz[n, 1] = odd
    fb = TAB["force_b"]
    fd = TAB["force_d"]
    along_b = contract(pressure, fb, 0)
    along_d = contract(pressure, fd, 0)
    bb = contract(along_b, fb, 1)
    fields = [
        contract(contract(along_d, fb, 1), fb, 2),
        contract(contract(along_b, fd, 1), fb, 2),
        contract(bb, fd, 2),
        contract(contract(contract(density, fb, 0), fb, 1), fb, 2),
    ]
    for f in FIELDS:
        for a in TRIPLE:
            for b in TRIPLE:
                parts[f, 3 * a + b, 0] = fields[f][a, b, 0] + sh.z_prev(fields[f][a, b, 2])
                parts[f, 3 * a + b, 1] = fields[f][a, b, 1]
    lists = []
    for high, trace in ((True, "high_trace"), (False, "low_trace")):
        values = side_values(rho, 0, TAB[trace])
        for f in FIELDS:
            for b in TRIPLE:
                for z in PAIR:
                    line = [parts[f, 3 * a + b, z] for a in TRIPLE]
                    if high:
                        line[0] = line[0] + roll_rows(line[2], 2)
                    else:
                        line[2] = line[2] + roll_rows(line[0], -2)
                    for a in TRIPLE:
                        values["sum", f, a, b, z] = line[a]
        for d in TRIPLE:
            for p in PAIR:
                for z in PAIR:
                    first = vz[4 * d + p, z]
                    values["old", d, 0, p, z] = first
                    values["old", d, 1, p, z] = vz[4 * d + 2 + p, z]
                    values["old", d, 2, p, z] = roll_rows(first, -2)
        lists.append([values[key] for key in x_keys(high)])
    write_messages(sh, even_along(GX), near, far, *lists, 2)


def assemble(sh, own, side, step):
    inner = [own[0] + sh.before(side[2], own[2], step), own[1], own[2] + sh.before(own[0], side[0], step)]
    outer = [
        jnp.where(sh.first[step], side[0] + roll_rows(own[2], -step), side[0]),
        side[1],
        jnp.where(sh.first[step], side[2], side[2] + roll_rows(own[0], step)),
    ]
    return inner, outer


def rim_kernel(
    parts, vz, rho, from_far, from_near,
    sums, sums_x, old, old_x, rho_x, heat_x, near, far,
):
    sh = Shifts()
    left, right = read_messages(
        sh, even_along(GX), from_near, from_far, x_keys(True), x_keys(False), 2
    )

    def beside(*key):
        return sh.beside(right(key), left(key), 2)

    for f in FIELDS:
        for b in TRIPLE:
            for z in PAIR:
                own = [parts[f, 3 * a + b, z] for a in TRIPLE]
                side = [beside("sum", f, a, b, z) for a in TRIPLE]
                inner, outer = assemble(sh, own, side, 2)
                for a in TRIPLE:
                    sums[f, 3 * a + b, z] = inner[a]
                    sums_x[f, 3 * a + b, z] = outer[a]
    for d in TRIPLE:
        for p in PAIR:
            for z in PAIR:
                first = vz[4 * d + p, z]
                beyond = beside("old", d, 0, p, z)
                old[d, p, z] = first
                old[d, 2 + p, z] = vz[4 * d + 2 + p, z]
                old[d, 4 + p, z] = sh.before(first, beyond, 2)
                old_x[d, p, z] = beyond
                old_x[d, 2 + p, z] = beside("old", d, 1, p, z)
                old_x[d, 4 + p, z] = sh.beside(right(("old", d, 2, p, z)), roll_rows(first, 2), 2)
    for key in POINTS:
        rho_x[point(*key)] = beside("rho", *key)
    for m in TRIPLE:
        for n in TRIPLE:
            heat_x[3 * m + n] = beside("heat", m, n)
    lists = []
    for high, trace in ((True, "high_trace"), (False, "low_trace")):
        values = side_values(rho, 1, TAB[trace])
        for f in FIELDS:
            for a in TRIPLE:
                for z in PAIR:
                    line = [sums[f, 3 * a + b, z] for b in TRIPLE]
                    if high:
                        line[0] = line[0] + roll_rows(line[2], 1)
                    else:
                        line[2] = line[2] + roll_rows(line[0], -1)
                    for b in TRIPLE:
                        values["sum", f, a, b, z] = line[b]
        for f in FIELDS:
            b = 2 if high else 0
            for z in PAIR:
                values["side", f, "mid", z] = sums_x[f, 3 + b, z]
                values["side", f, "far", z] = sh.beside(sums_x[f, 6 + b, z], sums_x[f, b, z], 2)
        for d in TRIPLE:
            for a in TRIPLE:
                for z in PAIR:
                    first = old[d, 2 * a, z]
                    values["old", d, a, 0, z] = first
                    values["old", d, a, 1, z] = old[d, 2 * a + 1, z]
                    values["old", d, a, 2, z] = roll_rows(first, -1)
            for z in PAIR:
                values["old_side", d, "mid", z] = old_x[d, 2, z]
                values["old_side", d, "far", z] = sh.beside(old_x[d, 4, z], old_x[d, 0, z], 2)
        lists.append([values[key] for key in y_keys(high)])
    write_messages(sh, even_along(GY), near, far, *lists, 1)


FACE_KEYS = [(f, m) for f in range(5) for m in range(9)]


def velocity_kernel(
    scale, sums, sums_x, old, old_x, rho, rho_x, heat_x, from_far, from_near,
    stored, u0, disp, speeds, sides, split, wide, new_vel, sem,
):
    sh = Shifts()
    lane = lane_index()
    step = scale[...]
    down, up = read_messages(
        sh, even_along(GY), from_near, from_far, y_keys(True), y_keys(False), 1
    )

    def beside(*key):
        return sh.beside(up(key), down(key), 1)

    def aside_of(get, kind, a, own, f, z):
        if a == 1:
            return get((kind, f, "mid", z))
        far = get((kind, f, "far", z))
        if a == 0:
            return sh.beside(roll_rows(own(2), -2), far, 2)
        return sh.beside(far, roll_rows(own(0), 2), 2)

    centre = [{} for _ in TRIPLE]
    side_x = [{} for _ in TRIPLE]
    side_y = [{} for _ in TRIPLE]
    for a in TRIPLE:
        for z in PAIR:
            total = []
            for f in FIELDS:
                own = [sums[f, 3 * a + b, z] for b in TRIPLE]
                inner, outer = assemble(sh, own, [beside("sum", f, a, b, z) for b in TRIPLE], 1)
                aside = [sums_x[f, 3 * a + b, z] for b in TRIPLE]
                aside = [
                    aside[0] + sh.before(
                        aside_of(down, "side", a, lambda n: down(("sum", f, n, 2, z)), f, z),
                        aside[2],
                        1,
                    ),
                    aside[1],
                    aside[2] + sh.before(
                        aside[0],
                        aside_of(up, "side", a, lambda n: up(("sum", f, n, 0, z)), f, z),
                        1,
                    ),
                ]
                total.append((inner, aside, outer))
            for d in TRIPLE:
                first = old[d, 2 * a, z]
                first_x = old_x[d, 2 * a, z]
                beyond = beside("old", d, a, 0, z)
                olds = (
                    [first, old[d, 2 * a + 1, z], sh.before(first, beyond, 1)],
                    [
                        first_x,
                        old_x[d, 2 * a + 1, z],
                        sh.before(
                            first_x,
                            aside_of(up, "old_side", a, lambda n: up(("old", d, n, 0, z)), d, z),
                            1,
                        ),
                    ],
                    [
                        beyond,
                        beside("old", d, a, 1, z),
                        sh.beside(up(("old", d, a, 2, z)), roll_rows(first, 1), 1),
                    ],
                )
                for kind, target in enumerate((centre, side_x, side_y)):
                    for b in TRIPLE:
                        over_mass = step / total[3][kind][b]
                        target[d][a, b, z] = olds[kind][b] + total[d][kind][b] * over_mass
    vel = centre
    for d in range(3):
        for px in range(2):
            slot = 2 * d + px
            for py in range(2):
                even = vel[d][px, py, 0]
                odd = vel[d][px, py, 1]
                tile = jnp.where(row_index() < 4, even, roll_rows(odd, 4))
                split[slot, pl.ds(py, 8, stride=2), :] = tile
            even = split[slot, 0:8, :]
            odd = split[slot, 8:16, :]
            for part in range(2):
                at = 64 * part + lane // 2
                wide[slot, :, 128 * part : 128 * part + 128] = jnp.where(
                    (lane & 1) == 0,
                    jnp.take_along_axis(even, at, axis=1),
                    jnp.take_along_axis(odd, at, axis=1),
                )
            new_vel[d, px] = wide[slot, 0:4, :]
            new_vel[d, 2 + px] = wide[slot, 4:8, :]
    store = pltpu.make_async_copy(new_vel, stored, sem)
    store.start()
    eb = TAB["eval_b"]
    minus = -step

    def along_z(even, odd):
        line = [even, odd, sh.z_next(even)]
        return [combine(line, column(eb, q)) for q in range(3)]

    def at_points(nodes, own):
        gauss = [{} for _ in range(3)]
        for d in range(3):
            across = {}
            for b in range(3):
                for z in range(2):
                    line = [nodes[d][a, b, z] for a in range(3)]
                    for q in range(3):
                        across[q, b, z] = combine(line, column(eb, q))
            if d == 1 and own:
                for b, at in ((0, 2), (2, 3)):
                    for q in range(3):
                        for c, value in enumerate(along_z(across[q, b, 0], across[q, b, 1])):
                            speeds[at, 3 * q + c] = minus * value
            for qx in range(3):
                for qy in range(3):
                    pair = [
                        combine([across[qx, b, z] for b in range(3)], column(eb, qy))
                        for z in range(2)
                    ]
                    if d == 2 and own:
                        speeds[4, 3 * qx + qy] = minus * pair[0]
                    for c, value in enumerate(along_z(*pair)):
                        gauss[d][qx, qy, c] = value
                        if own:
                            disp[d, point(qx, qy, c)] = minus * value
        return gauss

    for a, at in ((0, 0), (2, 1)):
        for q in range(3):
            pair = [combine([vel[0][a, b, z] for b in range(3)], column(eb, q)) for z in range(2)]
            for c, value in enumerate(along_z(*pair)):
                speeds[at, 3 * q + c] = minus * value
    gauss = at_points(centre, True)
    for q in range(27):
        u0[0, q] = rho[0, q]
        u0[1, q] = rho[1, q]
    for d in range(3):
        for key in POINTS:
            u0[2 + d, point(*key)] = rho[0, point(*key)] * gauss[d][key]
    low = TAB["low_trace"]
    high = TAB["high_trace"]
    for side, nodes in enumerate((side_x, side_y)):
        turn = 2 - side
        gauss = at_points(nodes, False)
        trace = [jnp.where(sh.first[turn], low[a], high[a]) for a in TRIPLE]
        weigh = {}
        for key in POINTS:
            dens = beside("rho", *key) if side else rho_x[point(*key)]
            weigh[key] = trace[key[side]] * dens
        for m in TRIPLE:
            for n in TRIPLE:
                keys = [(a, m, n) if side == 0 else (m, a, n) for a in TRIPLE]
                at = 3 * m + n
                sides[side, 0, at] = weigh[keys[0]] + weigh[keys[1]] + weigh[keys[2]]
                sides[side, 1, at] = beside("heat", m, n) if side else heat_x[at]
                for d in TRIPLE:
                    sides[side, 2 + d, at] = sum(weigh[k] * gauss[d][k] for k in keys)
    store.wait()


def stage_kernel(weight, last, *refs):
    refs = list(refs)
    u0 = refs.pop(0)
    u = u0 if weight is None else refs.pop(0)
    disp, speeds = refs[:2]
    sh = Shifts()
    even = [even_along(GX), even_along(GY)]
    if weight is None:
        sides = refs[2]
        outs = refs[3:]
    else:
        outs = refs[6:]
        if last:
            sems = outs.pop()
            ready = outs.pop()
        sides = outs.pop()
        for d in range(2):
            step = 2 - d
            near, far = (refs[2 + ORDER.index((k, d))] for k in ("near", "far"))
            under, over = read_messages(sh, even[d], near, far, FACE_KEYS, FACE_KEYS, step)
            for f, m in FACE_KEYS:
                sides[d, f, m] = sh.beside(over((f, m)), under((f, m)), step)
    traces = None if last else outs.pop()
    lift = TAB["low_lift"]
    volume = TAB["volume"]
    odd_w = 0.5 * (volume[0][0] - volume[2][0])
    even_w = 0.5 * (volume[0][0] + volume[2][0])
    odd_f = 0.5 * (lift[0] + lift[2])
    even_f = 0.5 * (lift[0] - lift[2])

    def one_field(f, carry):
        fields = {key: u[f, point(*key)] for key in POINTS}
        rate = {}
        for d in range(3):
            for m in range(3):
                for n in range(3):
                    if d == 0:
                        keys = [(a, m, n) for a in range(3)]
                    elif d == 1:
                        keys = [(m, a, n) for a in range(3)]
                    else:
                        keys = [(m, n, a) for a in range(3)]
                    at = 3 * m + n
                    line = [fields[k] for k in keys]
                    moved = [disp[d, point(*k)] * fields[k] for k in keys]
                    tm, tp = both_traces(line)
                    if d < 2:
                        step = 2 - d
                        before = sh.before(sides[d, f, at], tp, step)
                        after = sh.before(tm, sides[d, f, at], step)
                        s_low = speeds[2 * d, at]
                        s_high = speeds[2 * d + 1, at]
                        f_low = s_low * jnp.where(s_low > 0.0, before, tm)
                        f_high = s_high * jnp.where(s_high > 0.0, tp, after)
                    else:
                        s_low = speeds[4, at]
                        f_low = s_low * jnp.where(s_low > 0.0, sh.z_prev(tp), tm)
                        f_high = sh.z_next(f_low)
                    across = moved[0] - moved[2]
                    jump = f_low - f_high
                    odd = odd_w * across + odd_f * jump
                    even_part = even_w * (moved[0] + moved[2]) + volume[1][0] * moved[1]
                    even_part = even_part + even_f * (f_low + f_high)
                    pieces = [
                        odd + even_part,
                        volume[0][1] * across + lift[1] * jump,
                        odd - even_part,
                    ]
                    for k, piece in zip(keys, pieces):
                        rate[k] = rate[k] + piece if d else piece
        after = {}
        for key in POINTS:
            q = point(*key)
            if weight is None:
                value = fields[key] + rate[key]
            else:
                value = (1.0 - weight) * u0[f, q] + weight * (fields[key] + rate[key])
            if last:
                ready[f, q, 0] = value[0:2]
                ready[f, q, 1] = value[2:4]
            else:
                outs[0][f, q] = value
                after[key] = value
        if last:
            pltpu.make_async_copy(ready.at[f], outs[0].at[f], sems.at[f]).start()
        else:
            for d in range(2):
                for m in range(3):
                    for n in range(3):
                        keys = [(a, m, n) if d == 0 else (m, a, n) for a in range(3)]
                        tm, tp = both_traces([after[k] for k in keys])
                        traces[2 * d, f, 3 * m + n] = tp
                        traces[2 * d + 1, f, 3 * m + n] = tm
        return carry

    lax.fori_loop(0, 5, one_field, 0, unroll=True)
    if last:
        for f in range(5):
            pltpu.make_async_copy(ready.at[f], outs[0].at[f], sems.at[f]).wait()
    else:
        for d in range(2):
            lists = [[traces[2 * d + k, f, m] for f, m in FACE_KEYS] for k in range(2)]
            write_messages(sh, even[d], outs[1 + 2 * d], outs[2 + 2 * d], *lists, 2 - d)


def velocity_stage_kernel(*refs):
    operands, results, stage, scratch = refs[:10], refs[10:14], refs[14:19], refs[19:]
    sides, *work, traces = scratch
    velocity_kernel(*operands, *results, sides, *work)
    stage_kernel(None, False, *results[1:], sides, *stage, traces)


def call(kernel, outs, *args, scratch=(), name=None, weigh=None, far=False, stored=()):
    space = pltpu.HBM if far else pltpu.VMEM
    return pl.pallas_call(
        kernel,
        out_shape=[jax.ShapeDtypeStruct(o, F32) for o in outs],
        in_specs=[pl.BlockSpec(memory_space=space) for _ in args],
        out_specs=[
            pl.BlockSpec(memory_space=pltpu.HBM if n in stored else pltpu.VMEM)
            for n in range(len(outs))
        ],
        scratch_shapes=[pltpu.VMEM(s, F32) if isinstance(s, tuple) else s for s in scratch],
        compiler_params=pltpu.CompilerParams(vmem_limit_bytes=(60 if far else 32) * 1024 * 1024),
        cost_estimate=weigh,
        name=name,
    )(*args)


def axis_count(axes):
    return math.prod(lax.axis_size(axis) for axis in axes)


def near_swap(value, axis):
    return lax.ppermute(value, axis, [(i, i ^ 1) for i in range(axis_count(axis))])


def far_swap(value, axis):
    count = axis_count(axis)
    return lax.ppermute(value, axis, [(i, (i + 2 * (i % 2) - 1) % count) for i in range(count)])


def exchange(near_x, far_x, near_y, far_y):
    received = {
        ("near", 0): near_swap(near_x, GX),
        ("far", 0): far_swap(far_x, GX),
        ("near", 1): near_swap(near_y, GY),
        ("far", 1): far_swap(far_y, GY),
    }
    return [received[key] for key in ORDER]


def shards(density, energy, velocity):
    tile = TILE
    dens = density.reshape((27,) + density.shape[3:])
    ener = energy.reshape((27,) + energy.shape[3:])
    arranged = [(27,) + tile, (12,) + tile, (6, 8, 256), (6, 16, 128)]
    near, far, top = call(
        pack_kernel,
        [(3,) + tile, (3,) + tile, (axis_count(FIRST), 128)],
        dens, ener, velocity,
        scratch=[dens.shape, ener.shape, velocity.shape] + arranged + [pltpu.SemaphoreType.DMA((3,))],
        far=True,
        name="pack",
    )
    far = far_swap(far, GZ)
    near = near_swap(near, GZ)
    tops = lax.all_to_all(top, FIRST, 0, 0, tiled=True)
    (top,) = call(top_kernel, [(axis_count(SECOND), 128)], tops, name="top", weigh=WEIGHT)
    tops = lax.all_to_all(top, SECOND, 0, 0, tiled=True)
    (step,) = call(step_kernel, [tile], tops, name="step", weigh=WEIGHT)
    parts_shape = (4, 9, 2) + tile
    old_shape = (3, 6, 2) + tile
    message = (message_size(x_keys(True), x_keys(False)),) + tile
    rho, vz, parts, near, far = call(
        force_kernel,
        [(2, 27) + tile, (12, 2) + tile, parts_shape, message, message],
        dens, ener, velocity, far, near,
        scratch=arranged,
        name="force",
    )
    far = far_swap(far, GX)
    near = near_swap(near, GX)
    message = (message_size(y_keys(True), y_keys(False)),) + tile
    sums, sums_x, old, old_x, rho_x, heat_x, near, far = call(
        rim_kernel,
        [
            parts_shape, parts_shape, old_shape, old_shape, (27,) + tile, (9,) + tile,
            message, message,
        ],
        parts, vz, rho, far, near,
        name="rim",
    )
    far = far_swap(far, GY)
    near = near_swap(near, GY)
    state = (5, 27) + tile
    faces = [(message_size(FACE_KEYS),) + tile] * 4
    held = (4, 5, 9) + tile
    sides = (2, 5, 9) + tile
    new_velocity, u0, disp, speeds, one, *messages = call(
        velocity_stage_kernel,
        [velocity.shape, state, (3, 27) + tile, (5, 9) + tile, state] + faces,
        step, sums, sums_x, old, old_x, rho, rho_x, heat_x, far, near,
        scratch=[
            sides, (6, 16, 128), (6, 8, 256), velocity.shape, pltpu.SemaphoreType.DMA, held,
        ],
        stored=(0,),
        name="velocity_stage_one",
    )
    two, *messages = call(
        functools.partial(stage_kernel, 0.25, False), [state] + faces,
        u0, one, disp, speeds, *exchange(*messages),
        scratch=[held, sides],
        name="stage_two",
    )
    (remapped,) = call(
        functools.partial(stage_kernel, 2.0 / 3.0, True), [(5, 27) + density.shape[3:]],
        u0, two, disp, speeds, *exchange(*messages),
        scratch=[sides, (5, 27) + density.shape[3:], pltpu.SemaphoreType.DMA((5,))],
        stored=(0,),
        name="stage_three",
    )
    return new_velocity, remapped.reshape((5, 3, 3, 3) + density.shape[3:])


def solution(mesh):
    across, high, deep = (mesh.shape[axis] for axis in ("gx", "gy", "gz"))
    devices = mesh.devices.reshape(across, high // 2, 2, 2, deep // 2)
    return jax.shard_map(
        shards,
        mesh=Mesh(devices, GX + GY + GZ),
        in_specs=(
            P(None, None, None, GX, GY, GZ),
            P(None, None, None, GX, GY, GZ),
            P(None, GX, GY, GZ),
        ),
        out_specs=(P(None, GX, GY, GZ), P(None, None, None, None, GX, GY, GZ)),
        check_vma=False,
    )
```
